256 devices in a mesh: dp: 2 (over y_lo), spatial: 4 (over x), code: 32 (over z, y_hi, core).
Axes of the slice: x: 4, y: 4 (y_hi: 2, y_lo: 2; y = y_hi * 2 + y_lo), z: 8, core: 2. Of those that a mesh axis runs over, the one named last changes fastest.
Arguments:
- features: bfloat16 [8, 16, 16, 512], P('dp', 'spatial'), may hold values from -28 to 28
- conv_weight: bfloat16 [3, 3, 512, 256], replicated, may hold values from -0.09375 to 0.09375
- codebook: float32 [131072, 256], P('code'), may hold values from -1 to 1
- recon_grad: bfloat16 [8, 16, 16, 256], P('dp', 'spatial'), may hold values from -6 to 6
Outputs:
- codebook_grad: float32 [131072, 256], P('code', 'dp')
- feature_grad: bfloat16 [8, 16, 16, 512], P('dp', 'spatial')
The draws below stay inside these ranges and needn't reach their ends.
All inputs are finite; a program needn't handle non-finite values.
Results may differ from the reference program's by a relative error of at most 0.0065.
Values may be sent and summed in bfloat16 or wider, within the bound.
A program may use at most 128 MiB of HBM per device.

```python
import jax
import jax.numpy as jnp
from jax import lax

D = 256
CIN = 512
CODES_DEV = 4096
CODES = 131072
LH = 16
LW = 16
IMAGES = 8
LATENTS = 2048
N_CODE = 32


def draw_features(key, part):
    key = jax.random.fold_in(key, 7)
    value_key = jax.random.fold_in(key, 1)
    shape = (IMAGES, LH, LW, CIN)
    values = jnp.clip(jax.random.normal(value_key, shape, jnp.float32), -4.0, 4.0)
    return values.astype(jnp.bfloat16)


def levels(key, dims, cuts, low, top_value):
    gain, own = 1.0, jax.random.fold_in(key, 6)
    for position, shards_of in cuts:
        steps = jnp.exp(jax.random.uniform(jax.random.fold_in(own, position), (shards_of,), jnp.float32, low / len(cuts), top_value / len(cuts)))
        gain = gain * jnp.repeat(steps, dims[position] // shards_of).reshape([-1 if axis == position else 1 for axis in range(len(dims))])
    return gain


def centred(own_key, extent, scale, limit, cuts=(), held_as=jnp.bfloat16):
    level = levels(own_key, extent, cuts, -0.22, 0.18) if cuts else 1.0
    entries = jax.random.normal(own_key, extent, jnp.float32) * scale * level
    return jnp.minimum(jnp.maximum(entries, -limit), limit).astype(held_as)


def setup_inputs(seed: int = 0) -> dict:
    splits = jax.random.split(jax.random.key(seed), 5)
    return {
        "features": draw_features(jax.random.fold_in(splits[4], 71), 0),
        "conv_weight": centred(splits[1], (3, 3, CIN, D), (9 * CIN) ** -0.5, 0.09375),
        "codebook": centred(splits[2], (CODES, D), (D // 9) ** -0.5, 1.0, ((0, 32),), jnp.float32),
        "recon_grad": centred(splits[3], (IMAGES, LH, LW, D), 1.0, 6.0, ((0, 2), (1, 4))),
    }


def convolve(inputs, kernel):
    return lax.conv_general_dilated(inputs, kernel, (1, 1), ((1, 1), (1, 1)), dimension_numbers=("NHWC", "HWIO", "NHWC"), preferred_element_type=jnp.float32)


def reference(features, conv_weight, codebook, recon_grad):
    highest = lax.Precision.HIGHEST
    latent = convolve(features, conv_weight)
    latent_rows = latent.reshape(-1, D)
    upstream = recon_grad.reshape(-1, D).astype(jnp.float32)
    code_blocks = codebook.reshape(N_CODE, CODES_DEV, D)

    def scores_of(code_block):
        return jnp.dot(latent_rows, code_block.T, precision=highest)

    block_maxima = lax.map(lambda code_block: jnp.max(scores_of(code_block), axis=1), code_blocks)
    top_score = jnp.max(block_maxima, axis=0)

    def mass_parts(code_block):
        weights = jnp.exp(scores_of(code_block) - top_score[:, None])
        return jnp.sum(weights, axis=1), jnp.dot(weights, code_block, precision=highest)

    block_mass, block_sums = lax.map(mass_parts, code_blocks)
    mass_total = jnp.sum(block_mass, axis=0)
    reconstructed = jnp.sum(block_sums, axis=0) / mass_total[:, None]
    inner_dot = jnp.sum(upstream * reconstructed, axis=1)

    def backward(carry, code_block):
        probabilities = jnp.exp(scores_of(code_block) - top_score[:, None]) / mass_total[:, None]
        projected = jnp.dot(upstream, code_block.T, precision=highest)
        grad_scores = probabilities * (projected - inner_dot[:, None])
        block_grad = jnp.dot(probabilities.T, upstream, precision=highest) + jnp.dot(grad_scores.T, latent_rows, precision=highest)
        carry = carry + jnp.dot(grad_scores, code_block, precision=highest)
        return carry, block_grad

    latent_total, block_grads = lax.scan(backward, jnp.zeros((latent_rows.shape[0], D), jnp.float32), code_blocks)
    codebook_grad = block_grads.reshape(CODES, D) * (CODES / LATENTS)
    latent_grad = latent_total.astype(jnp.bfloat16).reshape(latent.shape)
    flipped = jnp.transpose(conv_weight[::-1, ::-1], (0, 1, 3, 2))
    feature_grad = convolve(latent_grad, flipped).astype(jnp.bfloat16)
    return codebook_grad, feature_grad
```

```python
import functools

import jax
import jax.numpy as jnp
from jax import lax
from jax.experimental import pallas as pl
from jax.experimental.pallas import tpu as pltpu
from jax.sharding import PartitionSpec as P

MESH = pl.DeviceIdType.MESH
BF = jnp.bfloat16
F32 = jnp.float32
NX, NY, NZ = 4, 4, 8
IMG, BAND, LW, CIN, D = 4, 4, 16, 512, 256
ROWS = IMG * BAND * LW
CODES = 4096
HALF = CODES // 2
BLK = HALF // NX
OWN = IMG * BAND * LW // 4
HD = D // 2
EDGE_SEMS = 8


def nt(a, b):
    return lax.dot_general(a, b, (((1,), (1,)), ((), ())), preferred_element_type=F32)


def nn(a, b):
    return lax.dot_general(a, b, (((1,), (0,)), ((), ())), preferred_element_type=F32)


def tn(a, b):
    return lax.dot_general(a, b, (((0,), (0,)), ((), ())), preferred_element_type=F32)


def shifted(acc, step):
    rows = acc.shape[0]
    col = lax.broadcasted_iota(jnp.int32, acc.shape, 0) % LW
    keep = (col >= 1) if step == 1 else (col < LW - 1)
    return jnp.where(keep, pltpu.roll(acc, step % rows, 0), 0.0)


def kernel(
    feat, cw_hbm, cb_hbm, up,
    cg, fg,
    xp, cw, cb, hi, lo, right, lat_lo, wts, proj, mst, pg, gb,
    st, st_col, st_z, snd, rcv, own, fin,
    gsum, g_col, gz_src, g_z, lg_src, lg,
    l_sem, h_ss, h_rs, u_ss, u_rs, t_ss, t_rs, sc_ss, sc_rs, sz_ss, sz_rs,
    r_ss, r_rs, a_ss, a_rs, gc_ss, gc_rs, gz_ss, gz_rs, lg_ss, lg_rs, e_ss, e_rs,
):
    d, s, k = lax.axis_index("dp"), lax.axis_index("spatial"), lax.axis_index("code")
    z, yh, c = k // 4, (k // 2) % 2, k % 2
    y = yh * 2 + d

    def dev(x_, y_, z_, c_):
        return (y_ % 2, x_, z_ * 4 + (y_ // 2) * 2 + c_)

    def xdev(o):
        return dev((s + o) % NX, y, z, c)

    def ydev(j):
        return dev(s, (y + j) % NY, z, c)

    def coldev(i):
        return dev(s, (y + i // 2) % NY, z, (c + i) % 2)

    def zdev(i):
        return dev(s, y, (z + i) % NZ, c)

    def agdev(f, o):
        return ((d + f) % 2, (s + o) % NX, k)

    def edgedev(e, i):
        return dev((s + e) % NX, (y + 2 * (i // 2)) % NY, z, (c + i) % 2)

    def remote(src, dst, ss, rs, who):
        return pltpu.make_async_remote_copy(
            src_ref=src, dst_ref=dst, send_sem=ss, recv_sem=rs,
            device_id=who, device_id_type=MESH,
        )

    load_cb = pltpu.make_async_copy(cb_hbm.at[pl.ds(d * HALF, HALF)], cb, l_sem.at[0])
    load_u = pltpu.make_async_copy(up, right.at[pl.ds(0, ROWS)], l_sem.at[1])
    load_x = pltpu.make_async_copy(feat, xp.at[:, pl.ds(1, BAND)], l_sem.at[2])
    load_w = pltpu.make_async_copy(cw_hbm, cw, l_sem.at[3])
    barrier = pltpu.get_barrier_semaphore()
    peers = [xdev(o) for o in range(1, NX)] + [coldev(i) for i in range(1, 8)]
    peers += [zdev(i) for i in range(1, NZ)] + [agdev(1, o) for o in range(1, NX)]
    peers += [edgedev(e, i) for e in (1, NX - 1) for i in range(1, 4)]
    for who in peers:
        pl.semaphore_signal(barrier, inc=1, device_id=who, device_id_type=MESH)
    load_cb.start()
    load_u.start()
    load_x.start()
    load_w.start()
    load_cb.wait()

    @pl.loop(0, HALF // 256)
    def _(i):
        rows = pl.ds(pl.multiple_of(i * 256, 256), 256)
        v = cb[rows, :]
        h = v.astype(BF)
        hi[rows, :] = h
        lo[rows, :] = (v - h.astype(F32)).astype(BF)

    pl.semaphore_wait(barrier, len(peers))

    halo = [
        remote(feat.at[:, BAND - 1], xp.at[:, 0], h_ss.at[0], h_rs.at[0], xdev(1)),
        remote(feat.at[:, 0], xp.at[:, BAND + 1], h_ss.at[1], h_rs.at[1], xdev(NX - 1)),
    ]
    hrows = ROWS // 2
    give_u = [
        remote(
            up.at[pl.ds(n * hrows, hrows)], right.at[pl.ds(ROWS + n * hrows, hrows)],
            u_ss.at[n], u_rs.at[n], ydev((1, 3)[n]),
        )
        for n in range(2)
    ]
    for cp in halo + give_u:
        cp.start()

    def project(rb):
        u = right[rb * ROWS:(rb + 1) * ROWS, :]

        @pl.loop(0, NX)
        def _(i):
            rows = pl.ds(pl.multiple_of(i * BLK, BLK), BLK)
            proj[rows, rb * ROWS:(rb + 1) * ROWS] = nt(hi[rows, :], u) + nt(lo[rows, :], u)

    load_u.wait()
    project(0)

    load_x.wait()
    load_w.wait()
    for cp in halo:
        cp.wait_recv()

    @pl.when(s == 0)
    def _():
        xp[:, 0] = jnp.zeros((IMG, LW, CIN), BF)

    @pl.when(s == NX - 1)
    def _():
        xp[:, BAND + 1] = jnp.zeros((IMG, LW, CIN), BF)

    def taps(b):
        acc = None
        for a in range(3):
            xa = xp[:, a:a + BAND].reshape(ROWS, CIN)
            t = nn(xa, cw[a, b])
            acc = t if acc is None else acc + t
        return acc

    latent = taps(1) + shifted(taps(0), 1) + shifted(taps(2), -1)
    lat_hi = latent.astype(BF)
    right[2 * ROWS:3 * ROWS, :] = lat_hi
    lat_lo[:ROWS, :] = (latent - lat_hi.astype(F32)).astype(BF)
    give_t = []
    for n in range(2):
        rows = pl.ds(2 * ROWS + n * hrows, hrows)
        to = pl.ds(3 * ROWS + n * hrows, hrows)
        give_t.append(remote(right.at[rows], right.at[to], t_ss.at[n], t_rs.at[n], ydev((1, 3)[n])))
        rows = pl.ds(n * hrows, hrows)
        to = pl.ds(ROWS + n * hrows, hrows)
        give_t.append(remote(lat_lo.at[rows], lat_lo.at[to], t_ss.at[2 + n], t_rs.at[2 + n], ydev((1, 3)[n])))
    for cp in give_t:
        cp.start()

    def merge(a, b):
        top = jnp.maximum(a[0], b[0])
        ea, eb = jnp.exp(a[0] - top), jnp.exp(b[0] - top)
        return top, a[1] * ea + b[1] * eb, a[2] * ea + b[2] * eb

    def score(rb):
        cols = slice(rb * ROWS, (rb + 1) * ROWS)
        lh = right[(2 + rb) * ROWS:(3 + rb) * ROWS, :]
        ll = lat_lo[cols, :]

        def step(i, carry):
            rows = pl.ds(pl.multiple_of(i * BLK, BLK), BLK)
            h = hi[rows, :]
            sc = nt(h, lh) + (nt(h, ll) + nt(lo[rows, :], lh))
            top = jnp.max(sc, axis=0, keepdims=True)
            w = jnp.exp(sc - top)
            wts[rows, cols] = w
            mst[i, :, cols] = top
            mass = jnp.sum(w, axis=0, keepdims=True)
            dots = jnp.sum(w * proj[rows, cols], axis=0, keepdims=True)
            return merge(carry, (top, mass, dots))

        zero = jnp.zeros((1, ROWS), F32)
        top, mass, dots = lax.fori_loop(0, NX, step, (zero - 3.0e38, zero, zero))
        logs, mean = top + jnp.log(mass), dots / mass
        for n in range(2):
            st[2 * rb + n:2 * rb + n + 1, :] = logs[:, n * 128:(n + 1) * 128]
            st[4 + 2 * rb + n:5 + 2 * rb + n, :] = mean[:, n * 128:(n + 1) * 128]

    score(0)
    for cp in give_u:
        cp.wait_recv()
    project(1)
    for cp in give_t:
        cp.wait_recv()
    score(1)

    def combine(parts):
        top = functools.reduce(jnp.maximum, [p[:4] for p in parts])
        mass, dots = 0.0, 0.0
        for p in parts:
            e = jnp.exp(p[:4] - top)
            mass, dots = mass + e, dots + e * p[4:]
        return top + jnp.log(mass), dots / mass

    def swap(p):
        return jnp.concatenate([p[2:4], p[0:2], p[6:8], p[4:6]], axis=0)

    col = [remote(st, st_col.at[i - 1], sc_ss.at[i - 1], sc_rs.at[i - 1], coldev(i)) for i in range(1, 8)]
    for cp in col:
        cp.start()
    for cp in col:
        cp.wait_recv()
    parts = [st[...]]
    for i in range(1, 8):
        p = st_col[i - 1]
        parts.append(swap(p) if (i // 2) % 2 else p)
    logs, mean = combine(parts)
    st_z[0] = jnp.concatenate([logs, mean], axis=0)
    zs = [remote(st_z.at[0], st_z.at[i], sz_ss.at[i - 1], sz_rs.at[i - 1], zdev(i)) for i in range(1, NZ)]
    for cp in zs:
        cp.start()
    for cp in zs:
        cp.wait_recv()
    logs, mean = combine([st_z[i] for i in range(NZ)])
    total = jnp.concatenate([logs[n:n + 1] for n in range(4)], axis=1)
    inner = jnp.concatenate([mean[n:n + 1] for n in range(4)], axis=1)

    both = 2 * ROWS
    sums = []
    for o in (2, 1, 3, 0):
        blk = (s + o) % NX
        rows = pl.ds(pl.multiple_of(blk * BLK, BLK), BLK)
        p = wts[rows, :] * jnp.exp(mst[blk] - total)
        g = (p * (proj[rows, :] - inner)).astype(BF)
        pg[:, :both] = p.astype(BF)
        pg[:, both:] = g
        gb[rows, :] = g
        term = nn(pg[...], right[...])
        if o:
            snd[o - 1] = term.astype(BF)
            cp = remote(snd.at[o - 1], rcv.at[o - 1], r_ss.at[o - 1], r_rs.at[o - 1], xdev(o))
            cp.start()
            sums.append(cp)
        else:
            own[...] = term

    gsum[...] = tn(gb[...], hi[...]).astype(BF)

    def image(y_, c_):
        return (y_ // 2) * 2 + c_

    gcol = []
    for i in range(1, 8):
        j = i // 2
        base = (j % 2) * ROWS + image((y + j) % NY, (c + i) % 2) * OWN
        rows = pl.ds(pl.multiple_of(base, OWN), OWN)
        gcol.append(remote(gsum.at[rows], g_col.at[i - 1], gc_ss.at[i - 1], gc_rs.at[i - 1], coldev(i)))
    for cp in gcol:
        cp.start()
    for cp in gcol:
        cp.wait_recv()
    img = image(y, c)
    part = gsum[pl.ds(pl.multiple_of(img * OWN, OWN), OWN), :].astype(F32)
    for i in range(7):
        part = part + g_col[i].astype(F32)
    gz_src[...] = part.astype(BF)
    gzs = [remote(gz_src, g_z.at[i - 1], gz_ss.at[i - 1], gz_rs.at[i - 1], zdev(i)) for i in range(1, NZ)]
    for cp in gzs:
        cp.start()

    for cp in sums:
        cp.wait_recv()
    block = own[...]
    for o in range(3):
        block = block + rcv[o].astype(F32)
    left, rest = block[:, :HD].astype(BF), block[:, HD:].astype(BF)
    fin[0] = jnp.where(d == 0, left, rest)
    fin[1] = jnp.where(d == 0, rest, left)
    place = cg.at[pl.ds(pl.multiple_of(d * HALF + s * BLK, BLK), BLK)]
    out = []
    for f in (0, 1):
        for o in (2, 1, 3, 0):
            if f or o:
                n = f * NX + o
                out.append(remote(fin.at[f], place, a_ss.at[n], a_rs.at[n], agdev(f, o)))
    for cp in out:
        cp.start()
    keep = pltpu.make_async_copy(fin.at[0], place, l_sem.at[4])
    keep.start()

    for cp in gzs:
        cp.wait_recv()
    for i in range(NZ - 1):
        part = part + g_z[i].astype(F32)
    lg_src[...] = part.astype(BF).reshape(BAND, LW, D)
    lg[img, pl.ds(1, BAND)] = lg_src[...]
    back = []
    for n, i in enumerate((1, 4, 5)):
        back.append(remote(lg_src, lg.at[img, pl.ds(1, BAND)], lg_ss.at[n], lg_rs.at[n], coldev(i)))
    for n, (e, edge, to) in enumerate(((1, BAND - 1, 0), (NX - 1, 0, BAND + 1))):
        for i in range(4):
            m = n * 4 + i
            back.append(remote(lg_src.at[edge], lg.at[img, to], e_ss.at[m], e_rs.at[m], edgedev(e, i)))
    for cp in back:
        cp.start()
    for cp in back:
        cp.wait_recv()

    @pl.when(s == 0)
    def _():
        lg[:, 0] = jnp.zeros((IMG, LW, D), BF)

    @pl.when(s == NX - 1)
    def _():
        lg[:, BAND + 1] = jnp.zeros((IMG, LW, D), BF)

    def back_taps(b):
        acc = None
        for a in range(3):
            la = lg[:, 2 - a:2 - a + BAND].reshape(ROWS, D)
            t = nt(la, cw[a, b])
            acc = t if acc is None else acc + t
        return acc

    grad = back_taps(1) + shifted(back_taps(0), -1) + shifted(back_taps(2), 1)
    fg[...] = grad.astype(BF).reshape(IMG, BAND, LW, CIN)

    for cp in halo + give_u + give_t + col + zs + sums + gcol + gzs + back:
        cp.wait_send()
    keep.wait()
    for cp in out:
        cp.wait()


def on_device(features, conv_weight, codebook, recon_grad):
    dma = pltpu.SemaphoreType.DMA
    vm = pltpu.VMEM
    hbm = pl.BlockSpec(memory_space=pl.ANY)
    sems = [5, 2, 2, 2, 2, 4, 4, 7, 7, 7, 7, 3, 3, 8, 8, 7, 7, 7, 7, 3, 3, 8, 8]
    cg, fg = pl.pallas_call(
        kernel,
        out_shape=(
            jax.ShapeDtypeStruct((CODES, HD), BF),
            jax.ShapeDtypeStruct((IMG, BAND, LW, CIN), BF),
        ),
        in_specs=[hbm] * 4,
        out_specs=(hbm, pl.BlockSpec(memory_space=pltpu.VMEM)),
        scratch_shapes=[
            vm((IMG, BAND + 2, LW, CIN), BF),
            vm((3, 3, CIN, D), BF),
            vm((HALF, D), F32),
            vm((HALF, D), BF),
            vm((HALF, D), BF),
            vm((4 * ROWS, D), BF),
            vm((2 * ROWS, D), BF),
            vm((HALF, 2 * ROWS), F32),
            vm((HALF, 2 * ROWS), F32),
            vm((NX, 1, 2 * ROWS), F32),
            vm((BLK, 4 * ROWS), BF),
            vm((HALF, 2 * ROWS), BF),
            vm((8, 128), F32),
            vm((7, 8, 128), F32),
            vm((NZ, 8, 128), F32),
            vm((3, BLK, D), BF),
            vm((3, BLK, D), BF),
            vm((BLK, D), F32),
            vm((2, BLK, HD), BF),
            vm((2 * ROWS, D), BF),
            vm((7, OWN, D), BF),
            vm((OWN, D), BF),
            vm((NZ - 1, OWN, D), BF),
            vm((BAND, LW, D), BF),
            vm((IMG, BAND + 2, LW, D), BF),
        ] + [dma((n,)) for n in sems],
        compiler_params=pltpu.CompilerParams(
            collective_id=0, has_side_effects=True, vmem_limit_bytes=56 << 20
        ),
        cost_estimate=pl.CostEstimate(
            flops=12 * 2**30, bytes_accessed=10 << 20, transcendentals=1 << 21
        ),
        name="soft_quantize",
    )(features, conv_weight, codebook, recon_grad.reshape(ROWS, D))
    entries_all = codebook.shape[0] * lax.axis_size("code")
    rows_all = ROWS * lax.axis_size("dp") * lax.axis_size("spatial")
    return cg.astype(F32) * (entries_all / rows_all), fg


def solution(mesh):
    placed = (P("dp", "spatial", None, None), P(), P("code", None), P("dp", "spatial", None, None))
    return jax.shard_map(
        on_device,
        mesh=mesh,
        in_specs=placed,
        out_specs=(P("code", "dp"), P("dp", "spatial", None, None)),
        check_vma=False,
    )
```

```python
import functools

import jax
import jax.numpy as jnp
from jax import lax
from jax.experimental import pallas as pl
from jax.experimental.pallas import tpu as pltpu
from jax.sharding import PartitionSpec as P

MESH = pl.DeviceIdType.MESH
BF = jnp.bfloat16
F32 = jnp.float32
NX, NY, NZ = 4, 4, 8
IMG, BAND, LW, CIN, D = 4, 4, 16, 512, 256
ROWS = IMG * BAND * LW
CODES = 4096
HALF = CODES // 2
BLK = HALF // NX
OWN = IMG * BAND * LW // 4
HD = D // 2
EDGE_SEMS = 8


def nt(a, b):
    return lax.dot_general(a, b, (((1,), (1,)), ((), ())), preferred_element_type=F32)


def nn(a, b):
    return lax.dot_general(a, b, (((1,), (0,)), ((), ())), preferred_element_type=F32)


def tn(a, b):
    return lax.dot_general(a, b, (((0,), (0,)), ((), ())), preferred_element_type=F32)


def shifted(acc, step):
    rows = acc.shape[0]
    col = lax.broadcasted_iota(jnp.int32, acc.shape, 0) % LW
    keep = (col >= 1) if step == 1 else (col < LW - 1)
    return jnp.where(keep, pltpu.roll(acc, step % rows, 0), 0.0)


def kernel(
    feat, cw_hbm, cb_hbm, up,
    cg, fg,
    xp, cw, cb, hi, lo, right, lat_lo, wts, proj, mst, pg, gb,
    st, st_col, st_z, snd, rcv, own, fin,
    gsum, g_col, gz_src, g_z, lg_src, lg,
    l_sem, h_ss, h_rs, u_ss, u_rs, t_ss, t_rs, sc_ss, sc_rs, sz_ss, sz_rs,
    r_ss, r_rs, a_ss, a_rs, gc_ss, gc_rs, gz_ss, gz_rs, lg_ss, lg_rs, e_ss, e_rs, z_sem,
):
    d, s, k = lax.axis_index("dp"), lax.axis_index("spatial"), lax.axis_index("code")
    z, yh, c = k // 4, (k // 2) % 2, k % 2
    y = yh * 2 + d

    def dev(x_, y_, z_, c_):
        return (y_ % 2, x_, z_ * 4 + (y_ // 2) * 2 + c_)

    def xdev(o):
        return dev((s + o) % NX, y, z, c)

    def ydev(j):
        return dev(s, (y + j) % NY, z, c)

    def coldev(i):
        return dev(s, (y + i // 2) % NY, z, (c + i) % 2)

    def zdev(i):
        return dev(s, y, (z + i) % NZ, c)

    def agdev(f, o):
        return ((d + f) % 2, (s + o) % NX, k)

    def edgedev(e, i):
        return dev((s + e) % NX, (y + 2 * (i // 2)) % NY, z, (c + i) % 2)

    def remote(src, dst, ss, rs, who):
        return pltpu.make_async_remote_copy(
            src_ref=src, dst_ref=dst, send_sem=ss, recv_sem=rs,
            device_id=who, device_id_type=MESH,
        )

    load_cb = pltpu.make_async_copy(cb_hbm.at[pl.ds(d * HALF, HALF)], cb, l_sem.at[0])
    load_u = pltpu.make_async_copy(up, right.at[pl.ds(0, ROWS)], l_sem.at[1])
    load_x = pltpu.make_async_copy(feat, xp.at[:, pl.ds(1, BAND)], l_sem.at[2])
    load_w = pltpu.make_async_copy(cw_hbm, cw, l_sem.at[3])
    barrier = pltpu.get_barrier_semaphore()
    peers = [xdev(1), xdev(NX - 1), ydev(1), ydev(NY - 1), zdev(1), zdev(NZ - 1)]
    peers.append(dev(s, y, z, 1 - c))
    for who in peers:
        pl.semaphore_signal(barrier, inc=1, device_id=who, device_id_type=MESH)
    load_cb.start()
    load_u.start()
    load_x.start()
    load_w.start()
    load_cb.wait()

    @pl.loop(0, HALF // 256)
    def _(i):
        rows = pl.ds(pl.multiple_of(i * 256, 256), 256)
        v = cb[rows, :]
        h = v.astype(BF)
        hi[rows, :] = h
        lo[rows, :] = (v - h.astype(F32)).astype(BF)

    pl.semaphore_wait(barrier, len(peers))

    halo = [
        remote(feat.at[:, BAND - 1], xp.at[:, 0], h_ss.at[0], h_rs.at[0], xdev(1)),
        remote(feat.at[:, 0], xp.at[:, BAND + 1], h_ss.at[1], h_rs.at[1], xdev(NX - 1)),
    ]
    hrows = ROWS // 2
    give_u = [
        remote(
            up.at[pl.ds(n * hrows, hrows)], right.at[pl.ds(ROWS + n * hrows, hrows)],
            u_ss.at[n], u_rs.at[n], ydev((1, 3)[n]),
        )
        for n in range(2)
    ]
    for cp in halo + give_u:
        cp.start()

    def tell(n, reach):
        for i in (reach, NZ - reach):
            pl.semaphore_signal(z_sem.at[n], inc=1, device_id=zdev(i), device_id_type=MESH)

    tell(0, 1)

    def project(rb):
        u = right[rb * ROWS:(rb + 1) * ROWS, :]

        @pl.loop(0, NX)
        def _(i):
            rows = pl.ds(pl.multiple_of(i * BLK, BLK), BLK)
            proj[rows, rb * ROWS:(rb + 1) * ROWS] = nt(hi[rows, :], u) + nt(lo[rows, :], u)

    load_u.wait()
    project(0)

    load_x.wait()
    load_w.wait()
    for cp in halo:
        cp.wait_recv()

    @pl.when(s == 0)
    def _():
        xp[:, 0] = jnp.zeros((IMG, LW, CIN), BF)

    @pl.when(s == NX - 1)
    def _():
        xp[:, BAND + 1] = jnp.zeros((IMG, LW, CIN), BF)

    def taps(b):
        acc = None
        for a in range(3):
            xa = xp[:, a:a + BAND].reshape(ROWS, CIN)
            t = nn(xa, cw[a, b])
            acc = t if acc is None else acc + t
        return acc

    latent = taps(1) + shifted(taps(0), 1) + shifted(taps(2), -1)
    lat_hi = latent.astype(BF)
    right[2 * ROWS:3 * ROWS, :] = lat_hi
    lat_lo[:ROWS, :] = (latent - lat_hi.astype(F32)).astype(BF)
    pl.semaphore_wait(z_sem.at[0], 2)
    tell(1, 2)
    for cp in give_u:
        cp.wait_recv()
    give_t = []
    for n in range(2):
        rows = pl.ds(2 * ROWS + n * hrows, hrows)
        to = pl.ds(3 * ROWS + n * hrows, hrows)
        give_t.append(remote(right.at[rows], right.at[to], t_ss.at[n], t_rs.at[n], ydev((1, 3)[n])))
        rows = pl.ds(n * hrows, hrows)
        to = pl.ds(ROWS + n * hrows, hrows)
        give_t.append(remote(lat_lo.at[rows], lat_lo.at[to], t_ss.at[2 + n], t_rs.at[2 + n], ydev((1, 3)[n])))
    for cp in give_t:
        cp.start()

    def merge(a, b):
        top = jnp.maximum(a[0], b[0])
        ea, eb = jnp.exp(a[0] - top), jnp.exp(b[0] - top)
        return top, a[1] * ea + b[1] * eb, a[2] * ea + b[2] * eb

    def score(rb):
        cols = slice(rb * ROWS, (rb + 1) * ROWS)
        lh = right[(2 + rb) * ROWS:(3 + rb) * ROWS, :]
        ll = lat_lo[cols, :]

        def step(i, carry):
            rows = pl.ds(pl.multiple_of(i * BLK, BLK), BLK)
            h = hi[rows, :]
            sc = nt(h, lh) + (nt(h, ll) + nt(lo[rows, :], lh))
            top = jnp.max(sc, axis=0, keepdims=True)
            w = jnp.exp(sc - top)
            wts[rows, cols] = w
            mst[i, :, cols] = top
            mass = jnp.sum(w, axis=0, keepdims=True)
            dots = jnp.sum(w * proj[rows, cols], axis=0, keepdims=True)
            return merge(carry, (top, mass, dots))

        zero = jnp.zeros((1, ROWS), F32)
        top, mass, dots = lax.fori_loop(0, NX, step, (zero - 3.0e38, zero, zero))
        logs, mean = top + jnp.log(mass), dots / mass
        for n in range(2):
            st[2 * rb + n:2 * rb + n + 1, :] = logs[:, n * 128:(n + 1) * 128]
            st[4 + 2 * rb + n:5 + 2 * rb + n, :] = mean[:, n * 128:(n + 1) * 128]

    score(0)
    pl.semaphore_wait(z_sem.at[1], 2)
    project(1)
    for cp in give_t:
        cp.wait_recv()
    score(1)

    def combine(parts):
        top = functools.reduce(jnp.maximum, [p[:4] for p in parts])
        mass, dots = 0.0, 0.0
        for p in parts:
            e = jnp.exp(p[:4] - top)
            mass, dots = mass + e, dots + e * p[4:]
        return top + jnp.log(mass), dots / mass

    def swap(p):
        return jnp.concatenate([p[2:4], p[0:2], p[6:8], p[4:6]], axis=0)

    col = [remote(st, st_col.at[i - 1], sc_ss.at[i - 1], sc_rs.at[i - 1], coldev(i)) for i in range(1, 8)]
    for cp in col:
        cp.start()
    for cp in col:
        cp.wait_recv()
    parts = [st[...]]
    for i in range(1, 8):
        p = st_col[i - 1]
        parts.append(swap(p) if (i // 2) % 2 else p)
    logs, mean = combine(parts)
    st_z[0] = jnp.concatenate([logs, mean], axis=0)
    zs = [remote(st_z.at[0], st_z.at[i], sz_ss.at[i - 1], sz_rs.at[i - 1], zdev(i)) for i in range(1, NZ)]
    for cp in zs:
        cp.start()
    for cp in zs:
        cp.wait_recv()
    logs, mean = combine([st_z[i] for i in range(NZ)])
    total = jnp.concatenate([logs[n:n + 1] for n in range(4)], axis=1)
    inner = jnp.concatenate([mean[n:n + 1] for n in range(4)], axis=1)

    both = 2 * ROWS
    sums = []
    for o in (2, 1, 3, 0):
        blk = (s + o) % NX
        rows = pl.ds(pl.multiple_of(blk * BLK, BLK), BLK)
        p = wts[rows, :] * jnp.exp(mst[blk] - total)
        g = (p * (proj[rows, :] - inner)).astype(BF)
        pg[:, :both] = p.astype(BF)
        pg[:, both:] = g
        gb[rows, :] = g
        term = nn(pg[...], right[...])
        if o:
            snd[o - 1] = term.astype(BF)
            cp = remote(snd.at[o - 1], rcv.at[o - 1], r_ss.at[o - 1], r_rs.at[o - 1], xdev(o))
            cp.start()
            sums.append(cp)
        else:
            own[...] = term

    gsum[...] = tn(gb[...], hi[...]).astype(BF)

    def image(y_, c_):
        return (y_ // 2) * 2 + c_

    gcol = []
    for i in range(1, 8):
        j = i // 2
        base = (j % 2) * ROWS + image((y + j) % NY, (c + i) % 2) * OWN
        rows = pl.ds(pl.multiple_of(base, OWN), OWN)
        gcol.append(remote(gsum.at[rows], g_col.at[i - 1], gc_ss.at[i - 1], gc_rs.at[i - 1], coldev(i)))
    for cp in gcol:
        cp.start()
    for cp in gcol:
        cp.wait_recv()
    img = image(y, c)
    part = gsum[pl.ds(pl.multiple_of(img * OWN, OWN), OWN), :].astype(F32)
    for i in range(7):
        part = part + g_col[i].astype(F32)
    gz_src[...] = part.astype(BF)
    gzs = [remote(gz_src, g_z.at[i - 1], gz_ss.at[i - 1], gz_rs.at[i - 1], zdev(i)) for i in range(1, NZ)]
    for cp in gzs:
        cp.start()

    for cp in sums:
        cp.wait_recv()
    block = own[...]
    for o in range(3):
        block = block + rcv[o].astype(F32)
    left, rest = block[:, :HD].astype(BF), block[:, HD:].astype(BF)
    fin[0] = jnp.where(d == 0, left, rest)
    fin[1] = jnp.where(d == 0, rest, left)
    place = cg.at[pl.ds(pl.multiple_of(d * HALF + s * BLK, BLK), BLK)]
    out = []
    for f in (0, 1):
        for o in (2, 1, 3, 0):
            if f or o:
                n = f * NX + o
                out.append(remote(fin.at[f], place, a_ss.at[n], a_rs.at[n], agdev(f, o)))
    for cp in out:
        cp.start()
    keep = pltpu.make_async_copy(fin.at[0], place, l_sem.at[4])
    keep.start()

    for cp in gzs:
        cp.wait_recv()
    for i in range(NZ - 1):
        part = part + g_z[i].astype(F32)
    lg_src[...] = part.astype(BF).reshape(BAND, LW, D)
    lg[img, pl.ds(1, BAND)] = lg_src[...]
    back = []
    for n, i in enumerate((1, 4, 5)):
        back.append(remote(lg_src, lg.at[img, pl.ds(1, BAND)], lg_ss.at[n], lg_rs.at[n], coldev(i)))
    for n, (e, edge, to) in enumerate(((1, BAND - 1, 0), (NX - 1, 0, BAND + 1))):
        for i in range(4):
            m = n * 4 + i
            back.append(remote(lg_src.at[edge], lg.at[img, to], e_ss.at[m], e_rs.at[m], edgedev(e, i)))
    for cp in back:
        cp.start()
    for cp in back:
        cp.wait_recv()

    @pl.when(s == 0)
    def _():
        lg[:, 0] = jnp.zeros((IMG, LW, D), BF)

    @pl.when(s == NX - 1)
    def _():
        lg[:, BAND + 1] = jnp.zeros((IMG, LW, D), BF)

    def back_taps(b):
        acc = None
        for a in range(3):
            la = lg[:, 2 - a:2 - a + BAND].reshape(ROWS, D)
            t = nt(la, cw[a, b])
            acc = t if acc is None else acc + t
        return acc

    grad = back_taps(1) + shifted(back_taps(0), -1) + shifted(back_taps(2), 1)
    fg[...] = grad.astype(BF).reshape(IMG, BAND, LW, CIN)

    for cp in halo + give_u + give_t + col + zs + sums + gcol + gzs + back:
        cp.wait_send()
    keep.wait()
    for cp in out:
        cp.wait()


def finish_kernel(factor, cg, fg, out_cg, out_fg, got, wide, fgv, i_sem, o_sem):
    parts = got.shape[0]
    rows = CODES // parts
    take_fg = pltpu.make_async_copy(fg, fgv, i_sem.at[parts])
    takes, gives = [], []
    for n in range(parts):
        at = pl.ds(n * rows, rows)
        takes.append(pltpu.make_async_copy(cg.at[at], got.at[n], i_sem.at[n]))
        gives.append(pltpu.make_async_copy(wide.at[n], out_cg.at[at], o_sem.at[n]))
    gives.append(pltpu.make_async_copy(fgv, out_fg, o_sem.at[parts]))
    for cp in takes + [take_fg]:
        cp.start()
    for n in range(parts):
        takes[n].wait()
        wide[n] = got[n].astype(F32) * factor
        gives[n].start()
    take_fg.wait()
    gives[parts].start()
    for cp in gives:
        cp.wait()


def finish(cg, fg, factor):
    parts = 8
    hbm = pl.BlockSpec(memory_space=pl.ANY)
    return pl.pallas_call(
        functools.partial(finish_kernel, factor),
        out_shape=(
            jax.ShapeDtypeStruct(cg.shape, F32),
            jax.ShapeDtypeStruct(fg.shape, BF),
        ),
        in_specs=[hbm, hbm],
        out_specs=(hbm, hbm),
        scratch_shapes=[
            pltpu.VMEM((parts, CODES // parts, HD), BF),
            pltpu.VMEM((parts, CODES // parts, HD), F32),
            pltpu.VMEM(fg.shape, BF),
            pltpu.SemaphoreType.DMA((parts + 1,)),
            pltpu.SemaphoreType.DMA((parts + 1,)),
        ],
        compiler_params=pltpu.CompilerParams(vmem_limit_bytes=56 << 20),
        name="widen",
    )(cg, fg)


def on_device(features, conv_weight, codebook, recon_grad):
    dma = pltpu.SemaphoreType.DMA
    vm = pltpu.VMEM
    hbm = pl.BlockSpec(memory_space=pl.ANY)
    sems = [5, 2, 2, 2, 2, 4, 4, 7, 7, 7, 7, 3, 3, 8, 8, 7, 7, 7, 7, 3, 3, 8, 8]
    cg, fg = pl.pallas_call(
        kernel,
        out_shape=(
            jax.ShapeDtypeStruct((CODES, HD), BF),
            jax.ShapeDtypeStruct((IMG, BAND, LW, CIN), BF),
        ),
        in_specs=[hbm] * 4,
        out_specs=(hbm, pl.BlockSpec(memory_space=pltpu.VMEM)),
        scratch_shapes=[
            vm((IMG, BAND + 2, LW, CIN), BF),
            vm((3, 3, CIN, D), BF),
            vm((HALF, D), F32),
            vm((HALF, D), BF),
            vm((HALF, D), BF),
            vm((4 * ROWS, D), BF),
            vm((2 * ROWS, D), BF),
            vm((HALF, 2 * ROWS), F32),
            vm((HALF, 2 * ROWS), F32),
            vm((NX, 1, 2 * ROWS), F32),
            vm((BLK, 4 * ROWS), BF),
            vm((HALF, 2 * ROWS), BF),
            vm((8, 128), F32),
            vm((7, 8, 128), F32),
            vm((NZ, 8, 128), F32),
            vm((3, BLK, D), BF),
            vm((3, BLK, D), BF),
            vm((BLK, D), F32),
            vm((2, BLK, HD), BF),
            vm((2 * ROWS, D), BF),
            vm((7, OWN, D), BF),
            vm((OWN, D), BF),
            vm((NZ - 1, OWN, D), BF),
            vm((BAND, LW, D), BF),
            vm((IMG, BAND + 2, LW, D), BF),
        ] + [dma((n,)) for n in sems] + [pltpu.SemaphoreType.REGULAR((2,))],
        compiler_params=pltpu.CompilerParams(
            collective_id=0, has_side_effects=True, vmem_limit_bytes=56 << 20
        ),
        cost_estimate=pl.CostEstimate(
            flops=12 * 2**30, bytes_accessed=10 << 20, transcendentals=1 << 21
        ),
        name="soft_quantize",
    )(features, conv_weight, codebook, recon_grad.reshape(ROWS, D))
    entries_all = codebook.shape[0] * lax.axis_size("code")
    rows_all = ROWS * lax.axis_size("dp") * lax.axis_size("spatial")
    return finish(cg, fg, entries_all / rows_all)


def solution(mesh):
    placed = (P("dp", "spatial", None, None), P(), P("code", None), P("dp", "spatial", None, None))
    return jax.shard_map(
        on_device,
        mesh=mesh,
        in_specs=placed,
        out_specs=(P("code", "dp"), P("dp", "spatial", None, None)),
        check_vma=False,
    )
```

```python
import functools

import jax
import jax.numpy as jnp
from jax import lax
from jax.experimental import pallas as pl
from jax.experimental.pallas import tpu as pltpu
from jax.sharding import PartitionSpec as P

MESH = pl.DeviceIdType.MESH
BF = jnp.bfloat16
F32 = jnp.float32
NX, NY, NZ = 4, 4, 8
IMG, BAND, LW, CIN, D = 4, 4, 16, 512, 256
ROWS = IMG * BAND * LW
CODES = 4096
HALF = CODES // 2
BLK = HALF // NX
PART = BLK // 2
QTR = PART // 2
OWN = IMG * BAND * LW // 4
HD = D // 2


def nt(a, b):
    return lax.dot_general(a, b, (((1,), (1,)), ((), ())), preferred_element_type=F32)


def nn(a, b):
    return lax.dot_general(a, b, (((1,), (0,)), ((), ())), preferred_element_type=F32)


def tn(a, b):
    return lax.dot_general(a, b, (((0,), (0,)), ((), ())), preferred_element_type=F32)


def shifted(acc, step):
    rows = acc.shape[0]
    col = lax.broadcasted_iota(jnp.int32, acc.shape, 0) % LW
    keep = (col >= 1) if step == 1 else (col < LW - 1)
    return jnp.where(keep, pltpu.roll(acc, step % rows, 0), 0.0)


def kernel(
    feat, cw_hbm, cb_hbm, up,
    cg, fg,
    xp, cw, cb, hi, lo, right, lat_lo, wts, proj, mst, pg, gb,
    st, st_col, st_z, far, near, mid, got_far, got_left, got_right, own, fin,
    hi_t, gsum, g_col, gz_src, g_z, lg_src, lg,
    l_sem, h_ss, h_rs, u_ss, u_rs, t_ss, t_rs, sc_ss, sc_rs, sz_ss, sz_rs,
    r2_ss, r2_rs, rd_ss, rd_rs, rm_ss, rm_rs, a_ss, a_rs, gc_ss, gc_rs, gz_ss, gz_rs, lg_ss, lg_rs, e_ss, e_rs, z_sem,
):
    d, s, k = lax.axis_index("dp"), lax.axis_index("spatial"), lax.axis_index("code")
    z, yh, c = k // 4, (k // 2) % 2, k % 2
    y = yh * 2 + d

    def dev(x_, y_, z_, c_):
        return (y_ % 2, x_, z_ * 4 + (y_ // 2) * 2 + c_)

    def xdev(o):
        return dev((s + o) % NX, y, z, c)

    def ydev(j):
        return dev(s, (y + j) % NY, z, c)

    def coldev(i):
        return dev(s, (y + i // 2) % NY, z, (c + i) % 2)

    def zdev(i):
        return dev(s, y, (z + i) % NZ, c)

    def agdev(f, o):
        return ((d + f) % 2, (s + o) % NX, k)

    def edgedev(e, i):
        return dev((s + e) % NX, (y + 2 * (i // 2)) % NY, z, (c + i) % 2)

    def remote(src, dst, ss, rs, who):
        return pltpu.make_async_remote_copy(
            src_ref=src, dst_ref=dst, send_sem=ss, recv_sem=rs,
            device_id=who, device_id_type=MESH,
        )

    load_cb = pltpu.make_async_copy(cb_hbm.at[pl.ds(d * HALF, HALF)], cb, l_sem.at[0])
    load_u = pltpu.make_async_copy(up, right.at[pl.ds(0, ROWS)], l_sem.at[1])
    load_x = pltpu.make_async_copy(feat, xp.at[:, pl.ds(1, BAND)], l_sem.at[2])
    load_w = pltpu.make_async_copy(cw_hbm, cw, l_sem.at[3])
    barrier = pltpu.get_barrier_semaphore()
    peers = [xdev(1), xdev(NX - 1), ydev(1), ydev(NY - 1), zdev(1), zdev(NZ - 1)]
    peers.append(dev(s, y, z, 1 - c))
    for who in peers:
        pl.semaphore_signal(barrier, inc=1, device_id=who, device_id_type=MESH)
    load_cb.start()
    load_u.start()
    load_x.start()
    load_w.start()
    load_cb.wait()

    @pl.loop(0, HALF // 256)
    def _(i):
        rows = pl.ds(pl.multiple_of(i * 256, 256), 256)
        v = cb[rows, :]
        h = v.astype(BF)
        hi[rows, :] = h
        lo[rows, :] = (v - h.astype(F32)).astype(BF)

    pl.semaphore_wait(barrier, len(peers))

    halo = [
        remote(feat.at[:, BAND - 1], xp.at[:, 0], h_ss.at[0], h_rs.at[0], xdev(1)),
        remote(feat.at[:, 0], xp.at[:, BAND + 1], h_ss.at[1], h_rs.at[1], xdev(NX - 1)),
    ]
    hrows = ROWS // 2
    give_u = [
        remote(
            up.at[pl.ds(n * hrows, hrows)], right.at[pl.ds(ROWS + n * hrows, hrows)],
            u_ss.at[n], u_rs.at[n], ydev((1, 3)[n]),
        )
        for n in range(2)
    ]
    for cp in halo + give_u:
        cp.start()

    def tell(n, reach):
        for i in (reach, NZ - reach):
            pl.semaphore_signal(z_sem.at[n], inc=1, device_id=zdev(i), device_id_type=MESH)

    tell(0, 1)

    def project(rb):
        u = right[rb * ROWS:(rb + 1) * ROWS, :]

        @pl.loop(0, NX)
        def _(i):
            rows = pl.ds(pl.multiple_of(i * BLK, BLK), BLK)
            proj[rows, rb * ROWS:(rb + 1) * ROWS] = nt(hi[rows, :], u) + nt(lo[rows, :], u)

    load_u.wait()
    project(0)

    @pl.loop(0, HALF // 256)
    def _(i):
        at = pl.ds(pl.multiple_of(i * 256, 256), 256)
        hi_t[:, at] = hi[at, :].T


    load_x.wait()
    load_w.wait()
    for cp in halo:
        cp.wait_recv()

    @pl.when(s == 0)
    def _():
        xp[:, 0] = jnp.zeros((IMG, LW, CIN), BF)

    @pl.when(s == NX - 1)
    def _():
        xp[:, BAND + 1] = jnp.zeros((IMG, LW, CIN), BF)

    def taps(b):
        acc = None
        for a in range(3):
            xa = xp[:, a:a + BAND].reshape(ROWS, CIN)
            t = nn(xa, cw[a, b])
            acc = t if acc is None else acc + t
        return acc

    latent = taps(1) + shifted(taps(0), 1) + shifted(taps(2), -1)
    lat_hi = latent.astype(BF)
    right[2 * ROWS:3 * ROWS, :] = lat_hi
    lat_lo[:ROWS, :] = (latent - lat_hi.astype(F32)).astype(BF)
    pl.semaphore_wait(z_sem.at[0], 2)
    tell(1, 2)
    for cp in give_u:
        cp.wait_recv()
    give_t = []
    for n in range(2):
        rows = pl.ds(2 * ROWS + n * hrows, hrows)
        to = pl.ds(3 * ROWS + n * hrows, hrows)
        give_t.append(remote(right.at[rows], right.at[to], t_ss.at[n], t_rs.at[n], ydev((1, 3)[n])))
        rows = pl.ds(n * hrows, hrows)
        to = pl.ds(ROWS + n * hrows, hrows)
        give_t.append(remote(lat_lo.at[rows], lat_lo.at[to], t_ss.at[2 + n], t_rs.at[2 + n], ydev((1, 3)[n])))
    for cp in give_t:
        cp.start()

    def merge(a, b):
        top = jnp.maximum(a[0], b[0])
        ea, eb = jnp.exp(a[0] - top), jnp.exp(b[0] - top)
        return top, a[1] * ea + b[1] * eb, a[2] * ea + b[2] * eb

    def score(rb):
        cols = slice(rb * ROWS, (rb + 1) * ROWS)
        lh = right[(2 + rb) * ROWS:(3 + rb) * ROWS, :]
        ll = lat_lo[cols, :]

        def step(i, carry):
            rows = pl.ds(pl.multiple_of(i * BLK, BLK), BLK)
            h = hi[rows, :]
            sc = nt(h, lh) + (nt(h, ll) + nt(lo[rows, :], lh))
            top = jnp.max(sc, axis=0, keepdims=True)
            w = jnp.exp(sc - top)
            wts[rows, cols] = w
            mst[i, :, cols] = top
            mass = jnp.sum(w, axis=0, keepdims=True)
            dots = jnp.sum(w * proj[rows, cols], axis=0, keepdims=True)
            return merge(carry, (top, mass, dots))

        zero = jnp.zeros((1, ROWS), F32)
        top, mass, dots = lax.fori_loop(0, NX, step, (zero - 3.0e38, zero, zero))
        logs, mean = top + jnp.log(mass), dots / mass
        for n in range(2):
            st[2 * rb + n:2 * rb + n + 1, :] = logs[:, n * 128:(n + 1) * 128]
            st[4 + 2 * rb + n:5 + 2 * rb + n, :] = mean[:, n * 128:(n + 1) * 128]

    score(0)
    pl.semaphore_wait(z_sem.at[1], 2)
    project(1)
    for cp in give_t:
        cp.wait_recv()
    score(1)

    def combine(parts):
        top = functools.reduce(jnp.maximum, [p[:4] for p in parts])
        mass, dots = 0.0, 0.0
        for p in parts:
            e = jnp.exp(p[:4] - top)
            mass, dots = mass + e, dots + e * p[4:]
        return top + jnp.log(mass), dots / mass

    def swap(p):
        return jnp.concatenate([p[2:4], p[0:2], p[6:8], p[4:6]], axis=0)

    col = [remote(st, st_col.at[i - 1], sc_ss.at[i - 1], sc_rs.at[i - 1], coldev(i)) for i in range(1, 8)]
    for cp in col:
        cp.start()
    for cp in col:
        cp.wait_recv()
    parts = [st[...]]
    for i in range(1, 8):
        p = st_col[i - 1]
        parts.append(swap(p) if (i // 2) % 2 else p)
    logs, mean = combine(parts)
    st_z[0] = jnp.concatenate([logs, mean], axis=0)
    zs = [remote(st_z.at[0], st_z.at[i], sz_ss.at[i - 1], sz_rs.at[i - 1], zdev(i)) for i in range(1, NZ)]
    for cp in zs:
        cp.start()
    for cp in zs:
        cp.wait_recv()
    logs, mean = combine([st_z[i] for i in range(NZ)])
    total = jnp.concatenate([logs[n:n + 1] for n in range(4)], axis=1)
    inner = jnp.concatenate([mean[n:n + 1] for n in range(4)], axis=1)

    both = 2 * ROWS

    def term(o, h):
        blk = (s + o) % NX
        rows = pl.ds(pl.multiple_of(blk * BLK + h * PART, PART), PART)
        p = wts[rows, :] * jnp.exp(mst[blk] - total)
        g = (p * (proj[rows, :] - inner)).astype(BF)
        pg[:, :both] = p.astype(BF)
        pg[:, both:] = g
        gb[rows, :] = g
        return nn(pg[...], right[...])

    near_x = (1, NX - 1)
    first, second = slice(0, QTR), slice(QTR, PART)
    ring, direct, summed = [], [], []
    for h in range(2):
        t = term(2, h).astype(BF)
        for n, half in enumerate((first, second)):
            m = 2 * h + n
            far[m] = t[half]
            cp = remote(far.at[m], got_far.at[m], r2_ss.at[m], r2_rs.at[m], xdev(near_x[n]))
            cp.start()
            ring.append(cp)
        for n, (now, later) in enumerate(((second, first), (first, second))):
            m = 2 * h + n
            t = term(near_x[n], h)
            mid[m] = t[later]
            near[m, now] = t[now].astype(BF)
            at = pl.ds(now.start, QTR)
            to = (got_left, got_right)[n]
            cp = remote(near.at[m, at], to.at[h, at], rd_ss.at[m], rd_rs.at[m], xdev(near_x[n]))
            cp.start()
            direct.append(cp)
    for h in range(2):
        own[h] = term(0, h)
    gsum[...] = nn(hi_t[...], gb[...]).T.astype(BF)

    def image(y_, c_):
        return (y_ // 2) * 2 + c_

    gcol = []
    for i in range(1, 8):
        j = i // 2
        base = (j % 2) * ROWS + image((y + j) % NY, (c + i) % 2) * OWN
        rows = pl.ds(pl.multiple_of(base, OWN), OWN)
        gcol.append(remote(gsum.at[rows], g_col.at[i - 1], gc_ss.at[i - 1], gc_rs.at[i - 1], coldev(i)))
    for cp in gcol:
        cp.start()

    for h in range(2):
        for n, later in enumerate((first, second)):
            m = 2 * h + n
            ring[m].wait_recv()
            near[m, later] = (mid[m] + got_far[m].astype(F32)).astype(BF)
            at = pl.ds(later.start, QTR)
            to = (got_left, got_right)[n]
            cp = remote(near.at[m, at], to.at[h, at], rm_ss.at[m], rm_rs.at[m], xdev(near_x[n]))
            cp.start()
            summed.append(cp)

    out, keep = [], []

    def spread(h):
        for n in range(2):
            direct[2 * h + n].wait_recv()
            summed[2 * h + n].wait_recv()
        block = own[h] + got_left[h].astype(F32) + got_right[h].astype(F32)
        left, rest = block[:, :HD].astype(BF), block[:, HD:].astype(BF)
        fin[h, 0] = jnp.where(d == 0, left, rest)
        fin[h, 1] = jnp.where(d == 0, rest, left)
        place = cg.at[pl.ds(pl.multiple_of(d * HALF + s * BLK + h * PART, PART), PART)]
        for f in (0, 1):
            for o in (2, 1, 3, 0):
                if f or o:
                    n = h * 8 + f * NX + o
                    out.append(remote(fin.at[h, f], place, a_ss.at[n], a_rs.at[n], agdev(f, o)))
                    out[-1].start()
        keep.append(pltpu.make_async_copy(fin.at[h, 0], place, l_sem.at[4 + h]))
        keep[-1].start()

    spread(0)
    for cp in gcol:
        cp.wait_recv()
    img = image(y, c)
    part = gsum[pl.ds(pl.multiple_of(img * OWN, OWN), OWN), :].astype(F32)
    for i in range(7):
        part = part + g_col[i].astype(F32)
    gz_src[...] = part.astype(BF)
    gzs = [remote(gz_src, g_z.at[i - 1], gz_ss.at[i - 1], gz_rs.at[i - 1], zdev(i)) for i in range(1, NZ)]
    for cp in gzs:
        cp.start()
    spread(1)

    for cp in gzs:
        cp.wait_recv()
    for i in range(NZ - 1):
        part = part + g_z[i].astype(F32)
    lg_src[...] = part.astype(BF).reshape(BAND, LW, D)
    lg[img, pl.ds(1, BAND)] = lg_src[...]
    back = []
    for n, i in enumerate((1, 4, 5)):
        back.append(remote(lg_src, lg.at[img, pl.ds(1, BAND)], lg_ss.at[n], lg_rs.at[n], coldev(i)))
    for n, (e, edge, to) in enumerate(((1, BAND - 1, 0), (NX - 1, 0, BAND + 1))):
        for i in range(4):
            m = n * 4 + i
            back.append(remote(lg_src.at[edge], lg.at[img, to], e_ss.at[m], e_rs.at[m], edgedev(e, i)))
    for cp in back:
        cp.start()
    for cp in back:
        cp.wait_recv()

    @pl.when(s == 0)
    def _():
        lg[:, 0] = jnp.zeros((IMG, LW, D), BF)

    @pl.when(s == NX - 1)
    def _():
        lg[:, BAND + 1] = jnp.zeros((IMG, LW, D), BF)

    def back_taps(b):
        acc = None
        for a in range(3):
            la = lg[:, 2 - a:2 - a + BAND].reshape(ROWS, D)
            t = nt(la, cw[a, b])
            acc = t if acc is None else acc + t
        return acc

    grad = back_taps(1) + shifted(back_taps(0), -1) + shifted(back_taps(2), 1)
    fg[...] = grad.astype(BF).reshape(IMG, BAND, LW, CIN)

    for cp in halo + give_u + give_t + col + zs + ring + direct + summed + gcol + gzs + back:
        cp.wait_send()
    for cp in keep + out:
        cp.wait()


def finish_kernel(factor, cg, fg, out_cg, out_fg, got, wide, fgv, i_sem, o_sem):
    parts = got.shape[0]
    rows = CODES // parts
    take_fg = pltpu.make_async_copy(fg, fgv, i_sem.at[parts])
    takes, gives = [], []
    for n in range(parts):
        at = pl.ds(n * rows, rows)
        takes.append(pltpu.make_async_copy(cg.at[at], got.at[n], i_sem.at[n]))
        gives.append(pltpu.make_async_copy(wide.at[n], out_cg.at[at], o_sem.at[n]))
    gives.append(pltpu.make_async_copy(fgv, out_fg, o_sem.at[parts]))
    for cp in takes + [take_fg]:
        cp.start()
    for n in range(parts):
        takes[n].wait()
        wide[n] = got[n].astype(F32) * factor
        gives[n].start()
    take_fg.wait()
    gives[parts].start()
    for cp in gives:
        cp.wait()


def finish(cg, fg, factor):
    parts = 8
    hbm = pl.BlockSpec(memory_space=pl.ANY)
    return pl.pallas_call(
        functools.partial(finish_kernel, factor),
        out_shape=(
            jax.ShapeDtypeStruct(cg.shape, F32),
            jax.ShapeDtypeStruct(fg.shape, BF),
        ),
        in_specs=[hbm, hbm],
        out_specs=(hbm, hbm),
        scratch_shapes=[
            pltpu.VMEM((parts, CODES // parts, HD), BF),
            pltpu.VMEM((parts, CODES // parts, HD), F32),
            pltpu.VMEM(fg.shape, BF),
            pltpu.SemaphoreType.DMA((parts + 1,)),
            pltpu.SemaphoreType.DMA((parts + 1,)),
        ],
        compiler_params=pltpu.CompilerParams(vmem_limit_bytes=56 << 20),
        name="widen",
    )(cg, fg)


def on_device(features, conv_weight, codebook, recon_grad):
    dma = pltpu.SemaphoreType.DMA
    vm = pltpu.VMEM
    hbm = pl.BlockSpec(memory_space=pl.ANY)
    sems = [6, 2, 2, 2, 2, 4, 4, 7, 7, 7, 7, 4, 4, 4, 4, 4, 4, 16, 16, 7, 7, 7, 7, 3, 3, 8, 8]
    cg, fg = pl.pallas_call(
        kernel,
        out_shape=(
            jax.ShapeDtypeStruct((CODES, HD), BF),
            jax.ShapeDtypeStruct((IMG, BAND, LW, CIN), BF),
        ),
        in_specs=[hbm] * 4,
        out_specs=(hbm, pl.BlockSpec(memory_space=pltpu.VMEM)),
        scratch_shapes=[
            vm((IMG, BAND + 2, LW, CIN), BF),
            vm((3, 3, CIN, D), BF),
            vm((HALF, D), F32),
            vm((HALF, D), BF),
            vm((HALF, D), BF),
            vm((4 * ROWS, D), BF),
            vm((2 * ROWS, D), BF),
            vm((HALF, 2 * ROWS), F32),
            vm((HALF, 2 * ROWS), F32),
            vm((NX, 1, 2 * ROWS), F32),
            vm((PART, 4 * ROWS), BF),
            vm((HALF, 2 * ROWS), BF),
            vm((8, 128), F32),
            vm((7, 8, 128), F32),
            vm((NZ, 8, 128), F32),
            vm((4, QTR, D), BF),
            vm((4, PART, D), BF),
            vm((4, QTR, D), F32),
            vm((4, QTR, D), BF),
            vm((2, PART, D), BF),
            vm((2, PART, D), BF),
            vm((2, PART, D), F32),
            vm((2, 2, PART, HD), BF),
            vm((D, HALF), BF),
            vm((2 * ROWS, D), BF),
            vm((7, OWN, D), BF),
            vm((OWN, D), BF),
            vm((NZ - 1, OWN, D), BF),
            vm((BAND, LW, D), BF),
            vm((IMG, BAND + 2, LW, D), BF),
        ] + [dma((n,)) for n in sems] + [pltpu.SemaphoreType.REGULAR((2,))],
        compiler_params=pltpu.CompilerParams(
            collective_id=0, has_side_effects=True, vmem_limit_bytes=56 << 20
        ),
        cost_estimate=pl.CostEstimate(
            flops=12 * 2**30, bytes_accessed=10 << 20, transcendentals=1 << 21
        ),
        name="soft_quantize",
    )(features, conv_weight, codebook, recon_grad.reshape(ROWS, D))
    entries_all = codebook.shape[0] * lax.axis_size("code")
    rows_all = ROWS * lax.axis_size("dp") * lax.axis_size("spatial")
    return finish(cg, fg, entries_all / rows_all)


def solution(mesh):
    placed = (P("dp", "spatial", None, None), P(), P("code", None), P("dp", "spatial", None, None))
    return jax.shard_map(
        on_device,
        mesh=mesh,
        in_specs=placed,
        out_specs=(P("code", "dp"), P("dp", "spatial", None, None)),
        check_vma=False,
    )
```

```python
import functools

import jax
import jax.numpy as jnp
from jax import lax
from jax.experimental import pallas as pl
from jax.experimental.pallas import tpu as pltpu
from jax.sharding import PartitionSpec as P

MESH = pl.DeviceIdType.MESH
BF = jnp.bfloat16
F32 = jnp.float32
NX, NY, NZ = 4, 4, 8
IMG, BAND, LW, CIN, D = 4, 4, 16, 512, 256
ROWS = IMG * BAND * LW
CODES = 4096
HALF = CODES // 2
BLK = HALF // NX
PART = BLK // 2
QTR = PART // 2
OWN = IMG * LW
UNIT = OWN // LW
HD = D // 2


def nt(a, b):
    return lax.dot_general(a, b, (((1,), (1,)), ((), ())), preferred_element_type=F32)


def nn(a, b):
    return lax.dot_general(a, b, (((1,), (0,)), ((), ())), preferred_element_type=F32)


def tn(a, b):
    return lax.dot_general(a, b, (((0,), (0,)), ((), ())), preferred_element_type=F32)


def shifted(acc, step):
    rows = acc.shape[0]
    col = lax.broadcasted_iota(jnp.int32, acc.shape, 0) % LW
    keep = (col >= 1) if step == 1 else (col < LW - 1)
    return jnp.where(keep, pltpu.roll(acc, step % rows, 0), 0.0)


def kernel(
    feat, cw_hbm, cb_hbm, up,
    cg, fg,
    xp, cw, cb, hi, lo, right, lat_lo, wts, proj, mst, pg, wb, gb, sum_w, sum_g,
    st, st_col, st_z, far, near, mid, got_far, got_left, got_right, own, fin,
    hi_t, gsum, g_col, gz_src, g_z, lg_src, lg,
    l_sem, h_ss, h_rs, u_ss, u_rs, t_ss, t_rs, sc_ss, sc_rs, sz_ss, sz_rs,
    r2_ss, r2_rs, rd_ss, rd_rs, rm_ss, rm_rs, a_ss, a_rs, gc_ss, gc_rs, gz_ss, gz_rs, lg_ss, lg_rs, e_ss, e_rs, z_sem,
):
    d, s, k = lax.axis_index("dp"), lax.axis_index("spatial"), lax.axis_index("code")
    z, yh, c = k // 4, (k // 2) % 2, k % 2
    y = yh * 2 + d

    def dev(x_, y_, z_, c_):
        return (y_ % 2, x_, z_ * 4 + (y_ // 2) * 2 + c_)

    def xdev(o):
        return dev((s + o) % NX, y, z, c)

    def ydev(j):
        return dev(s, (y + j) % NY, z, c)

    def coldev(i):
        return dev(s, (y + i // 2) % NY, z, (c + i) % 2)

    def zdev(i):
        return dev(s, y, (z + i) % NZ, c)

    def agdev(f, o):
        return ((d + f) % 2, (s + o) % NX, k)

    def edgedev(e, i):
        return dev((s + e) % NX, (y + 2 * (i // 2)) % NY, z, (c + i) % 2)

    def remote(src, dst, ss, rs, who):
        return pltpu.make_async_remote_copy(
            src_ref=src, dst_ref=dst, send_sem=ss, recv_sem=rs,
            device_id=who, device_id_type=MESH,
        )

    load_cb = pltpu.make_async_copy(cb_hbm.at[pl.ds(d * HALF, HALF)], cb, l_sem.at[0])
    load_u = [
        pltpu.make_async_copy(up.at[:, h], right.at[pl.ds(h * UNIT, UNIT)], l_sem.at[4 + h])
        for h in range(BAND)
    ]
    load_x = [
        pltpu.make_async_copy(feat.at[:, h], xp.at[1 + h], l_sem.at[8 + h]) for h in range(BAND)
    ]
    load_w = pltpu.make_async_copy(cw_hbm, cw, l_sem.at[1])
    barrier = pltpu.get_barrier_semaphore()
    peers = [xdev(1), xdev(NX - 1), ydev(1), ydev(NY - 1), zdev(1), zdev(NZ - 1)]
    peers.append(dev(s, y, z, 1 - c))
    for who in peers:
        pl.semaphore_signal(barrier, inc=1, device_id=who, device_id_type=MESH)
    load_cb.start()
    for cp in load_x + [load_w] + load_u:
        cp.start()
    load_cb.wait()

    @pl.loop(0, HALF // 256)
    def _(i):
        rows = pl.ds(pl.multiple_of(i * 256, 256), 256)
        v = cb[rows, :]
        h = v.astype(BF)
        hi[rows, :] = h
        lo[rows, :] = (v - h.astype(F32)).astype(BF)

    pl.semaphore_wait(barrier, len(peers))

    for cp in load_u:
        cp.wait()
    halo = [
        remote(feat.at[:, BAND - 1], xp.at[0], h_ss.at[0], h_rs.at[0], xdev(1)),
        remote(feat.at[:, 0], xp.at[BAND + 1], h_ss.at[1], h_rs.at[1], xdev(NX - 1)),
    ]
    sides = (1, NY - 1)

    def share(buf, at, count, peer_at, ss, rs, n):
        return remote(
            buf.at[pl.ds(at, count)], buf.at[pl.ds(peer_at, count)], ss.at[n], rs.at[n], ydev(sides[n % 2])
        )

    quarter = ROWS // LW
    give_u = [
        share(right, n * 2 * UNIT, 2 * UNIT, quarter + n * 2 * UNIT, u_ss, u_rs, n) for n in range(2)
    ]
    for cp in halo + give_u:
        cp.start()

    def tell(n, reach):
        for i in (reach, NZ - reach):
            pl.semaphore_signal(z_sem.at[n], inc=1, device_id=zdev(i), device_id_type=MESH)

    tell(0, 1)

    def rows_of(buf, n):
        return buf[n * quarter:(n + 1) * quarter].reshape(ROWS, D)

    def project(rb):
        u = rows_of(right, rb)
        for i in range(NX):
            rows = slice(i * BLK, (i + 1) * BLK)
            proj[rows, rb * ROWS:(rb + 1) * ROWS] = nt(hi[rows, :], u) + nt(lo[rows, :], u)

    give_t = []

    def convolve(grid_rows):
        def taps(b):
            acc = None
            for a in range(3):
                xa = jnp.concatenate([xp[h + a].reshape(OWN, CIN) for h in grid_rows], axis=0)
                t = nn(xa, cw[a, b])
                acc = t if acc is None else acc + t
            return acc

        latent = taps(1) + shifted(taps(0), 1) + shifted(taps(2), -1)
        lat_hi = latent.astype(BF)
        rest = (latent - lat_hi.astype(F32)).astype(BF)
        for n, h in enumerate(grid_rows):
            at = slice(n * OWN, (n + 1) * OWN)
            right[2 * quarter + h * UNIT:2 * quarter + (h + 1) * UNIT] = lat_hi[at].reshape(UNIT, LW, D)
            lat_lo[h * UNIT:(h + 1) * UNIT] = rest[at].reshape(UNIT, LW, D)
        for n, h in enumerate(grid_rows):
            m = len(give_t)
            give_t.append(share(right, 2 * quarter + h * UNIT, UNIT, 3 * quarter + h * UNIT, t_ss, t_rs, m))
            give_t[-1].start()
        for n, h in enumerate(grid_rows):
            m = len(give_t)
            give_t.append(share(lat_lo, h * UNIT, UNIT, quarter + h * UNIT, t_ss, t_rs, m))
            give_t[-1].start()

    for cp in load_x + [load_w]:
        cp.wait()
    convolve((1, 2))
    project(0)

    @pl.loop(0, HALF // 256)
    def _(i):
        at = pl.ds(pl.multiple_of(i * 256, 256), 256)
        hi_t[:, at] = hi[at, :].T

    pl.semaphore_wait(z_sem.at[0], 2)
    tell(1, 2)
    for cp in halo + give_u:
        cp.wait_recv()

    @pl.when(s == 0)
    def _():
        xp[0] = jnp.zeros((IMG, LW, CIN), BF)

    @pl.when(s == NX - 1)
    def _():
        xp[BAND + 1] = jnp.zeros((IMG, LW, CIN), BF)

    convolve((0, BAND - 1))

    def merge(a, b):
        top = jnp.maximum(a[0], b[0])
        ea, eb = jnp.exp(a[0] - top), jnp.exp(b[0] - top)
        return top, a[1] * ea + b[1] * eb, a[2] * ea + b[2] * eb

    def score(rb):
        cols = slice(rb * ROWS, (rb + 1) * ROWS)
        lh = rows_of(right, 2 + rb)
        ll = rows_of(lat_lo, rb)

        def step(i, carry):
            rows = slice(i * BLK, (i + 1) * BLK)
            h = hi[rows, :]
            sc = nt(h, lh) + (nt(h, ll) + nt(lo[rows, :], lh))
            top = jnp.max(sc, axis=0, keepdims=True)
            w = jnp.exp(sc - top)
            wts[rows, cols] = w
            mst[i, :, cols] = top
            mass = jnp.sum(w, axis=0, keepdims=True)
            dots = jnp.sum(w * proj[rows, cols], axis=0, keepdims=True)
            return merge(carry, (top, mass, dots))

        zero = jnp.zeros((1, ROWS), F32)
        carry = (zero - 3.0e38, zero, zero)
        for i in range(NX):
            carry = step(i, carry)
        top, mass, dots = carry
        logs, mean = top + jnp.log(mass), dots / mass
        for n in range(2):
            st[2 * rb + n:2 * rb + n + 1, :] = logs[:, n * 128:(n + 1) * 128]
            st[4 + 2 * rb + n:5 + 2 * rb + n, :] = mean[:, n * 128:(n + 1) * 128]
        return logs, mean

    ends = [score(0)]
    pl.semaphore_wait(z_sem.at[1], 2)
    project(1)
    for cp in give_t:
        cp.wait_recv()
    ends.append(score(1))

    def combine(parts):
        top = functools.reduce(jnp.maximum, [p[:4] for p in parts])
        mass, dots = 0.0, 0.0
        for p in parts:
            e = jnp.exp(p[:4] - top)
            mass, dots = mass + e, dots + e * p[4:]
        return top + jnp.log(mass), dots / mass

    def swap(p):
        return jnp.concatenate([p[2:4], p[0:2], p[6:8], p[4:6]], axis=0)

    col = [remote(st, st_col.at[i - 1], sc_ss.at[i - 1], sc_rs.at[i - 1], coldev(i)) for i in range(1, 8)]
    for cp in col:
        cp.start()

    own_logs = jnp.concatenate([e[0] for e in ends], axis=1)
    own_mean = jnp.concatenate([e[1] for e in ends], axis=1)
    for i in range(2 * NX):
        rows = slice(i * PART, (i + 1) * PART)
        w = wts[rows, :] * jnp.exp(mst[i // 2] - own_logs)
        wb[rows, :] = w.astype(BF)
        gb[rows, :] = (w * (proj[rows, :] - own_mean)).astype(BF)
    sum_g[...] = nn(hi_t[...], gb[...])
    sum_w[...] = nn(hi_t[...], wb[...])

    for cp in col:
        cp.wait_recv()
    parts = [st[...]]
    for i in range(1, 8):
        p = st_col[i - 1]
        parts.append(swap(p) if (i // 2) % 2 else p)
    logs, mean = combine(parts)
    st_z[0] = jnp.concatenate([logs, mean], axis=0)
    zs = [remote(st_z.at[0], st_z.at[i], sz_ss.at[i - 1], sz_rs.at[i - 1], zdev(i)) for i in range(1, NZ)]
    for cp in zs:
        cp.start()
    for cp in zs:
        cp.wait_recv()
    logs, mean = combine([st_z[i] for i in range(NZ)])
    total = jnp.concatenate([logs[n:n + 1] for n in range(4)], axis=1)
    inner = jnp.concatenate([mean[n:n + 1] for n in range(4)], axis=1)

    both = 2 * ROWS

    def term(o, h):
        blk = (s + o) % NX
        rows = pl.ds(pl.multiple_of(blk * BLK + h * PART, PART), PART)
        p = wts[rows, :] * jnp.exp(mst[blk] - total)
        g = (p * (proj[rows, :] - inner)).astype(BF)
        pg[:, :both] = p.astype(BF)
        pg[:, both:] = g
        return nn(pg[...], right[...].reshape(4 * ROWS, D))

    share_of = jnp.exp(own_logs - total)
    gsum[...] = (share_of * (sum_g[...] + (own_mean - inner) * sum_w[...])).T.astype(BF)

    def grid_row(y_, c_):
        return (y_ // 2) * 2 + c_

    gcol = []
    for i in range(1, 8):
        j = i // 2
        base = (j % 2) * ROWS + grid_row((y + j) % NY, (c + i) % 2) * OWN
        rows = pl.ds(pl.multiple_of(base, OWN), OWN)
        gcol.append(remote(gsum.at[rows], g_col.at[i - 1], gc_ss.at[i - 1], gc_rs.at[i - 1], coldev(i)))

    near_x = (1, NX - 1)
    first, second = slice(0, QTR), slice(QTR, PART)
    ring, direct, summed = [], [], []
    for h in range(2):
        t = term(2, h).astype(BF)
        for n, half in enumerate((first, second)):
            m = 2 * h + n
            far[m] = t[half]
            cp = remote(far.at[m], got_far.at[m], r2_ss.at[m], r2_rs.at[m], xdev(near_x[n]))
            cp.start()
            ring.append(cp)
        for n, (now, later) in enumerate(((second, first), (first, second))):
            m = 2 * h + n
            t = term(near_x[n], h)
            mid[m] = t[later]
            near[m, now] = t[now].astype(BF)
            at = pl.ds(now.start, QTR)
            to = (got_left, got_right)[n]
            cp = remote(near.at[m, at], to.at[h, at], rd_ss.at[m], rd_rs.at[m], xdev(near_x[n]))
            cp.start()
            direct.append(cp)
    for cp in gcol:
        cp.start()
    for h in range(2):
        own[h] = term(0, h)
    for h in range(2):
        for n, later in enumerate((first, second)):
            m = 2 * h + n
            ring[m].wait_recv()
            near[m, later] = (mid[m] + got_far[m].astype(F32)).astype(BF)
            at = pl.ds(later.start, QTR)
            to = (got_left, got_right)[n]
            cp = remote(near.at[m, at], to.at[h, at], rm_ss.at[m], rm_rs.at[m], xdev(near_x[n]))
            cp.start()
            summed.append(cp)

    out, keep = [], []

    def spread(h):
        for n in range(2):
            direct[2 * h + n].wait_recv()
            summed[2 * h + n].wait_recv()
        block = own[h] + got_left[h].astype(F32) + got_right[h].astype(F32)
        left, rest = block[:, :HD].astype(BF), block[:, HD:].astype(BF)
        fin[h, 0] = jnp.where(d == 0, left, rest)
        fin[h, 1] = jnp.where(d == 0, rest, left)
        place = cg.at[pl.ds(pl.multiple_of(d * HALF + s * BLK + h * PART, PART), PART)]
        for f in (0, 1):
            for o in (2, 1, 3, 0):
                if f or o:
                    n = h * 8 + f * NX + o
                    out.append(remote(fin.at[h, f], place, a_ss.at[n], a_rs.at[n], agdev(f, o)))
                    out[-1].start()
        keep.append(pltpu.make_async_copy(fin.at[h, 0], place, l_sem.at[2 + h]))
        keep[-1].start()

    spread(0)
    for cp in gcol:
        cp.wait_recv()
    mine = grid_row(y, c)
    part = gsum[pl.ds(pl.multiple_of(mine * OWN, OWN), OWN), :].astype(F32)
    for i in range(7):
        part = part + g_col[i].astype(F32)
    gz_src[...] = part.astype(BF)
    gzs = [remote(gz_src, g_z.at[i - 1], gz_ss.at[i - 1], gz_rs.at[i - 1], zdev(i)) for i in range(1, NZ)]
    for cp in gzs:
        cp.start()
    spread(1)

    for cp in gzs:
        cp.wait_recv()
    for i in range(NZ - 1):
        part = part + g_z[i].astype(F32)
    lg_src[...] = part.astype(BF)
    lg[1 + mine] = lg_src[...]
    back = [
        remote(lg_src, lg.at[1 + mine], lg_ss.at[n], lg_rs.at[n], coldev(i))
        for n, i in enumerate((1, 4, 5))
    ]
    edges = []
    for n, (e, to) in enumerate(((1, 0), (NX - 1, BAND + 1))):
        edges.append([
            remote(lg_src, lg.at[to], e_ss.at[n * 4 + i], e_rs.at[n], edgedev(e, i)) for i in range(4)
        ])
    edge_row = (BAND - 1, 0)
    for n in range(2):

        @pl.when(mine == edge_row[n])
        def _():
            for cp in edges[n]:
                cp.start()

    for cp in back:
        cp.start()
    for cp in back + [edges[0][0], edges[1][0]]:
        cp.wait_recv()

    @pl.when(s == 0)
    def _():
        lg[0] = jnp.zeros((OWN, D), BF)

    @pl.when(s == NX - 1)
    def _():
        lg[BAND + 1] = jnp.zeros((OWN, D), BF)

    def back_taps(b):
        acc = None
        for a in range(3):
            la = lg[2 - a:2 - a + BAND].reshape(ROWS, D)
            t = nt(la, cw[a, b])
            acc = t if acc is None else acc + t
        return acc

    grad = back_taps(1) + shifted(back_taps(0), -1) + shifted(back_taps(2), 1)
    for h in range(BAND):
        fg[:, h] = grad[h * OWN:(h + 1) * OWN].astype(BF).reshape(IMG, LW, CIN)
    for n in range(2):

        @pl.when(mine == edge_row[n])
        def _():
            for cp in edges[n]:
                cp.wait_send()

    for cp in halo + give_u + give_t + col + zs + ring + direct + summed + gcol + gzs + back:
        cp.wait_send()
    for cp in keep + out:
        cp.wait()


def finish_kernel(factor, cg, fg, out_cg, out_fg, got, wide, fgv, i_sem, o_sem):
    parts = got.shape[0]
    rows = CODES // parts
    take_fg = pltpu.make_async_copy(fg, fgv, i_sem.at[parts])
    takes, gives = [], []
    for n in range(parts):
        at = pl.ds(n * rows, rows)
        takes.append(pltpu.make_async_copy(cg.at[at], got.at[n], i_sem.at[n]))
        gives.append(pltpu.make_async_copy(wide.at[n], out_cg.at[at], o_sem.at[n]))
    gives.append(pltpu.make_async_copy(fgv, out_fg, o_sem.at[parts]))
    for cp in takes + [take_fg]:
        cp.start()
    for n in range(parts):
        takes[n].wait()
        wide[n] = got[n].astype(F32) * factor
        gives[n].start()
    take_fg.wait()
    gives[parts].start()
    for cp in gives:
        cp.wait()


def finish(cg, fg, factor):
    parts = 8
    hbm = pl.BlockSpec(memory_space=pl.ANY)
    return pl.pallas_call(
        functools.partial(finish_kernel, factor),
        out_shape=(
            jax.ShapeDtypeStruct(cg.shape, F32),
            jax.ShapeDtypeStruct(fg.shape, BF),
        ),
        in_specs=[hbm, hbm],
        out_specs=(hbm, hbm),
        scratch_shapes=[
            pltpu.VMEM((parts, CODES // parts, HD), BF),
            pltpu.VMEM((parts, CODES // parts, HD), F32),
            pltpu.VMEM(fg.shape, BF),
            pltpu.SemaphoreType.DMA((parts + 1,)),
            pltpu.SemaphoreType.DMA((parts + 1,)),
        ],
        compiler_params=pltpu.CompilerParams(vmem_limit_bytes=56 << 20),
        name="widen",
    )(cg, fg)


def on_device(features, conv_weight, codebook, recon_grad):
    dma = pltpu.SemaphoreType.DMA
    vm = pltpu.VMEM
    hbm = pl.BlockSpec(memory_space=pl.ANY)
    sems = [12, 2, 2, 2, 2, 8, 8, 7, 7, 7, 7, 4, 4, 4, 4, 4, 4, 16, 16, 7, 7, 7, 7, 3, 3, 8, 2]
    cg, fg = pl.pallas_call(
        kernel,
        out_shape=(
            jax.ShapeDtypeStruct((CODES, HD), BF),
            jax.ShapeDtypeStruct((IMG, BAND, LW, CIN), BF),
        ),
        in_specs=[hbm] * 4,
        out_specs=(hbm, pl.BlockSpec(memory_space=pltpu.VMEM)),
        scratch_shapes=[
            vm((BAND + 2, IMG, LW, CIN), BF),
            vm((3, 3, CIN, D), BF),
            vm((HALF, D), F32),
            vm((HALF, D), BF),
            vm((HALF, D), BF),
            vm((4 * ROWS // LW, LW, D), BF),
            vm((2 * ROWS // LW, LW, D), BF),
            vm((HALF, 2 * ROWS), F32),
            vm((HALF, 2 * ROWS), F32),
            vm((NX, 1, 2 * ROWS), F32),
            vm((PART, 4 * ROWS), BF),
            vm((HALF, 2 * ROWS), BF),
            vm((HALF, 2 * ROWS), BF),
            vm((D, 2 * ROWS), F32),
            vm((D, 2 * ROWS), F32),
            vm((8, 128), F32),
            vm((7, 8, 128), F32),
            vm((NZ, 8, 128), F32),
            vm((4, QTR, D), BF),
            vm((4, PART, D), BF),
            vm((4, QTR, D), F32),
            vm((4, QTR, D), BF),
            vm((2, PART, D), BF),
            vm((2, PART, D), BF),
            vm((2, PART, D), F32),
            vm((2, 2, PART, HD), BF),
            vm((D, HALF), BF),
            vm((2 * ROWS, D), BF),
            vm((7, OWN, D), BF),
            vm((OWN, D), BF),
            vm((NZ - 1, OWN, D), BF),
            vm((OWN, D), BF),
            vm((BAND + 2, OWN, D), BF),
        ] + [dma((n,)) for n in sems] + [pltpu.SemaphoreType.REGULAR((2,))],
        compiler_params=pltpu.CompilerParams(
            collective_id=0, has_side_effects=True, vmem_limit_bytes=56 << 20
        ),
        cost_estimate=pl.CostEstimate(
            flops=12 * 2**30, bytes_accessed=10 << 20, transcendentals=1 << 21
        ),
        name="soft_quantize",
    )(features, conv_weight, codebook, recon_grad)
    entries_all = codebook.shape[0] * lax.axis_size("code")
    rows_all = ROWS * lax.axis_size("dp") * lax.axis_size("spatial")
    return finish(cg, fg, entries_all / rows_all)


def solution(mesh):
    placed = (P("dp", "spatial", None, None), P(), P("code", None), P("dp", "spatial", None, None))
    return jax.shard_map(
        on_device,
        mesh=mesh,
        in_specs=placed,
        out_specs=(P("code", "dp"), P("dp", "spatial", None, None)),
        check_vma=False,
    )
```

```python
import functools

import jax
import jax.numpy as jnp
from jax import lax
from jax.experimental import pallas as pl
from jax.experimental.pallas import tpu as pltpu
from jax.sharding import PartitionSpec as P

MESH = pl.DeviceIdType.MESH
BF = jnp.bfloat16
F32 = jnp.float32
NX, NY, NZ = 4, 4, 8
IMG, BAND, LW, CIN, D = 4, 4, 16, 512, 256
ROWS = IMG * BAND * LW
CODES = 4096
HALF = CODES // 2
BLK = HALF // NX
PART = BLK // 2
QTR = PART // 2
OWN = IMG * LW
UNIT = OWN // LW
HD = D // 2


def nt(a, b):
    return lax.dot_general(a, b, (((1,), (1,)), ((), ())), preferred_element_type=F32)


def nn(a, b):
    return lax.dot_general(a, b, (((1,), (0,)), ((), ())), preferred_element_type=F32)


def tn(a, b):
    return lax.dot_general(a, b, (((0,), (0,)), ((), ())), preferred_element_type=F32)


def shifted(acc, step):
    rows = acc.shape[0]
    col = lax.broadcasted_iota(jnp.int32, acc.shape, 0) % LW
    keep = (col >= 1) if step == 1 else (col < LW - 1)
    return jnp.where(keep, pltpu.roll(acc, step % rows, 0), 0.0)


def kernel(
    feat, cw_hbm, cb_hbm, up,
    cg, fg,
    xp, cw, cb, hi, lo, right, lat_lo, wts, proj, mst, pg, wb, gb, sum_w, sum_g,
    st, st_col, st_z, far, near, mid, got_far, got_left, got_right, own, fin,
    hi_t, gsum, g_col, gz_src, g_z, lg_src, lg,
    l_sem, h_ss, h_rs, u_ss, u_rs, t_ss, t_rs, sc_ss, sc_rs, sz_ss, sz_rs,
    r2_ss, r2_rs, rd_ss, rd_rs, rm_ss, rm_rs, a_ss, a_rs, gc_ss, gc_rs, gz_ss, gz_rs, lg_ss, lg_rs, e_ss, e_rs, z_sem,
):
    d, s, k = lax.axis_index("dp"), lax.axis_index("spatial"), lax.axis_index("code")
    z, yh, c = k // 4, (k // 2) % 2, k % 2
    y = yh * 2 + d

    def dev(x_, y_, z_, c_):
        return (y_ % 2, x_, z_ * 4 + (y_ // 2) * 2 + c_)

    def xdev(o):
        return dev((s + o) % NX, y, z, c)

    def ydev(j):
        return dev(s, (y + j) % NY, z, c)

    def coldev(i):
        return dev(s, (y + i // 2) % NY, z, (c + i) % 2)

    def zdev(i):
        return dev(s, y, (z + i) % NZ, c)

    def agdev(f, o):
        return ((d + f) % 2, (s + o) % NX, k)

    def edgedev(e, i):
        return dev((s + e) % NX, (y + 2 * (i // 2)) % NY, z, (c + i) % 2)

    def remote(src, dst, ss, rs, who):
        return pltpu.make_async_remote_copy(
            src_ref=src, dst_ref=dst, send_sem=ss, recv_sem=rs,
            device_id=who, device_id_type=MESH,
        )

    load_cb = pltpu.make_async_copy(cb_hbm.at[pl.ds(d * HALF, HALF)], cb, l_sem.at[0])
    load_u = [
        pltpu.make_async_copy(up.at[:, h], right.at[pl.ds(h * UNIT, UNIT)], l_sem.at[4 + h])
        for h in range(BAND)
    ]
    load_x = [
        pltpu.make_async_copy(feat.at[:, h], xp.at[1 + h], l_sem.at[8 + h]) for h in range(BAND)
    ]
    load_w = pltpu.make_async_copy(cw_hbm, cw, l_sem.at[1])
    barrier = pltpu.get_barrier_semaphore()
    peers = [xdev(1), xdev(NX - 1), ydev(1), ydev(NY - 1), zdev(1), zdev(NZ - 1)]
    peers.append(dev(s, y, z, 1 - c))
    for who in peers:
        pl.semaphore_signal(barrier, inc=1, device_id=who, device_id_type=MESH)
    load_cb.start()
    for cp in load_x + [load_w] + load_u:
        cp.start()
    load_cb.wait()

    @pl.loop(0, HALF // 256)
    def _(i):
        rows = pl.ds(pl.multiple_of(i * 256, 256), 256)
        v = cb[rows, :]
        h = v.astype(BF)
        hi[rows, :] = h
        lo[rows, :] = (v - h.astype(F32)).astype(BF)

    pl.semaphore_wait(barrier, len(peers))

    for cp in load_u:
        cp.wait()
    halo = [
        remote(feat.at[:, BAND - 1], xp.at[0], h_ss.at[0], h_rs.at[0], xdev(1)),
        remote(feat.at[:, 0], xp.at[BAND + 1], h_ss.at[1], h_rs.at[1], xdev(NX - 1)),
    ]
    sides = (1, NY - 1)

    def share(buf, at, count, peer_at, ss, rs, n):
        return remote(
            buf.at[pl.ds(at, count)], buf.at[pl.ds(peer_at, count)], ss.at[n], rs.at[n], ydev(sides[n % 2])
        )

    quarter = ROWS // LW
    give_u = [
        share(right, n * 2 * UNIT, 2 * UNIT, quarter + n * 2 * UNIT, u_ss, u_rs, n) for n in range(2)
    ]
    for cp in halo + give_u:
        cp.start()

    def tell(n, reach):
        for i in (reach, NZ - reach):
            pl.semaphore_signal(z_sem.at[n], inc=1, device_id=zdev(i), device_id_type=MESH)

    tell(0, 1)

    def rows_of(buf, n):
        return buf[n * quarter:(n + 1) * quarter].reshape(ROWS, D)

    def project(rb):
        u = rows_of(right, rb)
        for i in range(NX):
            rows = slice(i * BLK, (i + 1) * BLK)
            proj[rows, rb * ROWS:(rb + 1) * ROWS] = nt(hi[rows, :], u) + nt(lo[rows, :], u)

    give_t = []

    def convolve(grid_rows):
        def taps(b):
            acc = None
            for a in range(3):
                xa = jnp.concatenate([xp[h + a].reshape(OWN, CIN) for h in grid_rows], axis=0)
                t = nn(xa, cw[a, b])
                acc = t if acc is None else acc + t
            return acc

        latent = taps(1) + shifted(taps(0), 1) + shifted(taps(2), -1)
        lat_hi = latent.astype(BF)
        rest = (latent - lat_hi.astype(F32)).astype(BF)
        for n, h in enumerate(grid_rows):
            at = slice(n * OWN, (n + 1) * OWN)
            right[2 * quarter + h * UNIT:2 * quarter + (h + 1) * UNIT] = lat_hi[at].reshape(UNIT, LW, D)
            lat_lo[h * UNIT:(h + 1) * UNIT] = rest[at].reshape(UNIT, LW, D)
        for n, h in enumerate(grid_rows):
            m = len(give_t)
            give_t.append(share(right, 2 * quarter + h * UNIT, UNIT, 3 * quarter + h * UNIT, t_ss, t_rs, m))
            give_t[-1].start()
        for n, h in enumerate(grid_rows):
            m = len(give_t)
            give_t.append(share(lat_lo, h * UNIT, UNIT, quarter + h * UNIT, t_ss, t_rs, m))
            give_t[-1].start()

    for cp in load_x + [load_w]:
        cp.wait()
    convolve((1, 2))
    project(0)

    @pl.loop(0, HALF // 256)
    def _(i):
        at = pl.ds(pl.multiple_of(i * 256, 256), 256)
        hi_t[:, at] = hi[at, :].T

    pl.semaphore_wait(z_sem.at[0], 2)
    tell(1, 2)
    for cp in halo + give_u:
        cp.wait_recv()

    @pl.when(s == 0)
    def _():
        xp[0] = jnp.zeros((IMG, LW, CIN), BF)

    @pl.when(s == NX - 1)
    def _():
        xp[BAND + 1] = jnp.zeros((IMG, LW, CIN), BF)

    convolve((0, BAND - 1))

    def merge(a, b):
        top = jnp.maximum(a[0], b[0])
        ea, eb = jnp.exp(a[0] - top), jnp.exp(b[0] - top)
        return top, a[1] * ea + b[1] * eb, a[2] * ea + b[2] * eb

    def score(rb):
        cols = slice(rb * ROWS, (rb + 1) * ROWS)
        lh = rows_of(right, 2 + rb)
        ll = rows_of(lat_lo, rb)

        def step(i, carry):
            rows = slice(i * BLK, (i + 1) * BLK)
            h = hi[rows, :]
            sc = nt(h, lh) + (nt(h, ll) + nt(lo[rows, :], lh))
            top = jnp.max(sc, axis=0, keepdims=True)
            w = jnp.exp(sc - top)
            wts[rows, cols] = w
            mst[i, :, cols] = top
            mass = jnp.sum(w, axis=0, keepdims=True)
            dots = jnp.sum(w * proj[rows, cols], axis=0, keepdims=True)
            return merge(carry, (top, mass, dots))

        zero = jnp.zeros((1, ROWS), F32)
        carry = (zero - 3.0e38, zero, zero)
        for i in range(NX):
            carry = step(i, carry)
        top, mass, dots = carry
        logs, mean = top + jnp.log(mass), dots / mass
        for n in range(2):
            st[2 * rb + n:2 * rb + n + 1, :] = logs[:, n * 128:(n + 1) * 128]
            st[4 + 2 * rb + n:5 + 2 * rb + n, :] = mean[:, n * 128:(n + 1) * 128]
        return logs, mean

    ends = [score(0)]
    pl.semaphore_wait(z_sem.at[1], 2)
    project(1)
    for cp in give_t:
        cp.wait_recv()
    ends.append(score(1))

    def combine(parts):
        top = functools.reduce(jnp.maximum, [p[:4] for p in parts])
        mass, dots = 0.0, 0.0
        for p in parts:
            e = jnp.exp(p[:4] - top)
            mass, dots = mass + e, dots + e * p[4:]
        return top + jnp.log(mass), dots / mass

    def swap(p):
        return jnp.concatenate([p[2:4], p[0:2], p[6:8], p[4:6]], axis=0)

    col = [remote(st, st_col.at[i - 1], sc_ss.at[i - 1], sc_rs.at[i - 1], coldev(i)) for i in range(1, 8)]
    for cp in col:
        cp.start()

    own_logs = jnp.concatenate([e[0] for e in ends], axis=1)
    own_mean = jnp.concatenate([e[1] for e in ends], axis=1)
    for i in range(2 * NX):
        rows = slice(i * PART, (i + 1) * PART)
        w = wts[rows, :] * jnp.exp(mst[i // 2] - own_logs)
        wb[rows, :] = w.astype(BF)
        gb[rows, :] = (w * (proj[rows, :] - own_mean)).astype(BF)
    sum_g[...] = nn(hi_t[...], gb[...])
    sum_w[...] = nn(hi_t[...], wb[...])

    for cp in col:
        cp.wait_recv()
    parts = [st[...]]
    for i in range(1, 8):
        p = st_col[i - 1]
        parts.append(swap(p) if (i // 2) % 2 else p)
    logs, mean = combine(parts)
    st_z[0] = jnp.concatenate([logs, mean], axis=0)
    zs = [remote(st_z.at[0], st_z.at[i], sz_ss.at[i - 1], sz_rs.at[i - 1], zdev(i)) for i in range(1, NZ)]
    for cp in zs:
        cp.start()
    for cp in zs:
        cp.wait_recv()
    logs, mean = combine([st_z[i] for i in range(NZ)])
    total = jnp.concatenate([logs[n:n + 1] for n in range(4)], axis=1)
    inner = jnp.concatenate([mean[n:n + 1] for n in range(4)], axis=1)

    both = 2 * ROWS

    def term(o, h):
        blk = (s + o) % NX
        rows = pl.ds(pl.multiple_of(blk * BLK + h * PART, PART), PART)
        p = wts[rows, :] * jnp.exp(mst[blk] - total)
        g = (p * (proj[rows, :] - inner)).astype(BF)
        pg[:, :both] = p.astype(BF)
        pg[:, both:] = g
        return nn(pg[...], right[...].reshape(4 * ROWS, D))

    share_of = jnp.exp(own_logs - total)
    gsum[...] = (share_of * (sum_g[...] + (own_mean - inner) * sum_w[...])).T.astype(BF)

    def grid_row(y_, c_):
        return (y_ // 2) * 2 + c_

    gcol = []
    for i in range(1, 8):
        j = i // 2
        base = (j % 2) * ROWS + grid_row((y + j) % NY, (c + i) % 2) * OWN
        rows = pl.ds(pl.multiple_of(base, OWN), OWN)
        gcol.append(remote(gsum.at[rows], g_col.at[i - 1], gc_ss.at[i - 1], gc_rs.at[i - 1], coldev(i)))

    near_x = (1, NX - 1)
    first, second = slice(0, QTR), slice(QTR, PART)
    ring, direct, summed = [], [], []
    for h in range(2):
        t = term(2, h).astype(BF)
        for n, half in enumerate((first, second)):
            m = 2 * h + n
            far[m] = t[half]
            cp = remote(far.at[m], got_far.at[m], r2_ss.at[m], r2_rs.at[m], xdev(near_x[n]))
            cp.start()
            ring.append(cp)
        for n, (now, later) in enumerate(((second, first), (first, second))):
            m = 2 * h + n
            t = term(near_x[n], h)
            mid[m] = t[later]
            near[m, now] = t[now].astype(BF)
            at = pl.ds(now.start, QTR)
            to = (got_left, got_right)[n]
            cp = remote(near.at[m, at], to.at[h, at], rd_ss.at[m], rd_rs.at[m], xdev(near_x[n]))
            cp.start()
            direct.append(cp)
    for cp in gcol:
        cp.start()
    for h in range(2):
        own[h] = term(0, h)
    for h in range(2):
        for n, later in enumerate((first, second)):
            m = 2 * h + n
            ring[m].wait_recv()
            near[m, later] = (mid[m] + got_far[m].astype(F32)).astype(BF)
            at = pl.ds(later.start, QTR)
            to = (got_left, got_right)[n]
            cp = remote(near.at[m, at], to.at[h, at], rm_ss.at[m], rm_rs.at[m], xdev(near_x[n]))
            cp.start()
            summed.append(cp)

    for cp in gcol:
        cp.wait_recv()
    mine = grid_row(y, c)
    part = gsum[pl.ds(pl.multiple_of(mine * OWN, OWN), OWN), :].astype(F32)
    for i in range(7):
        part = part + g_col[i].astype(F32)
    gz_src[...] = part.astype(BF)
    gzs = [remote(gz_src, g_z.at[i - 1], gz_ss.at[i - 1], gz_rs.at[i - 1], zdev(i)) for i in range(1, NZ)]
    for cp in gzs:
        cp.start()

    out, keep = [], []

    def spread(h):
        for n in range(2):
            direct[2 * h + n].wait_recv()
            summed[2 * h + n].wait_recv()
        block = own[h] + got_left[h].astype(F32) + got_right[h].astype(F32)
        left, rest = block[:, :HD].astype(BF), block[:, HD:].astype(BF)
        fin[h, 0] = jnp.where(d == 0, left, rest)
        fin[h, 1] = jnp.where(d == 0, rest, left)
        place = cg.at[pl.ds(pl.multiple_of(d * HALF + s * BLK + h * PART, PART), PART)]
        for f in (0, 1):
            for o in (2, 1, 3, 0):
                if f or o:
                    n = h * 8 + f * NX + o
                    out.append(remote(fin.at[h, f], place, a_ss.at[n], a_rs.at[n], agdev(f, o)))
                    out[-1].start()
        keep.append(pltpu.make_async_copy(fin.at[h, 0], place, l_sem.at[2 + h]))
        keep[-1].start()

    spread(0)

    for cp in gzs:
        cp.wait_recv()
    for i in range(NZ - 1):
        part = part + g_z[i].astype(F32)
    lg_src[...] = part.astype(BF)
    lg[1 + mine] = lg_src[...]
    back = [
        remote(lg_src, lg.at[1 + mine], lg_ss.at[n], lg_rs.at[n], coldev(i))
        for n, i in enumerate((1, 4, 5))
    ]
    edges = []
    for n, (e, to) in enumerate(((1, 0), (NX - 1, BAND + 1))):
        edges.append([
            remote(lg_src, lg.at[to], e_ss.at[n * 4 + i], e_rs.at[n], edgedev(e, i)) for i in range(4)
        ])
    edge_row = (BAND - 1, 0)
    for n in range(2):

        @pl.when(mine == edge_row[n])
        def _():
            for cp in edges[n]:
                cp.start()

    for cp in back:
        cp.start()
    spread(1)
    for cp in back + [edges[0][0], edges[1][0]]:
        cp.wait_recv()

    @pl.when(s == 0)
    def _():
        lg[0] = jnp.zeros((OWN, D), BF)

    @pl.when(s == NX - 1)
    def _():
        lg[BAND + 1] = jnp.zeros((OWN, D), BF)

    def back_taps(b):
        acc = None
        for a in range(3):
            la = lg[2 - a:2 - a + BAND].reshape(ROWS, D)
            t = nt(la, cw[a, b])
            acc = t if acc is None else acc + t
        return acc

    grad = back_taps(1) + shifted(back_taps(0), -1) + shifted(back_taps(2), 1)
    for h in range(BAND):
        fg[:, h] = grad[h * OWN:(h + 1) * OWN].astype(BF).reshape(IMG, LW, CIN)
    for n in range(2):

        @pl.when(mine == edge_row[n])
        def _():
            for cp in edges[n]:
                cp.wait_send()

    for cp in halo + give_u + give_t + col + zs + ring + direct + summed + gcol + gzs + back:
        cp.wait_send()
    for cp in keep + out:
        cp.wait()


def finish_kernel(factor, cg, fg, out_cg, out_fg, wide, sem):
    parts = wide.shape[0]
    rows = CODES // parts
    gives = [pltpu.make_async_copy(fg, out_fg, sem.at[parts])]
    gives[0].start()
    for n in range(parts):
        at = pl.ds(n * rows, rows)
        wide[n] = cg[at, :].astype(F32) * factor
        gives.append(pltpu.make_async_copy(wide.at[n], out_cg.at[at], sem.at[n]))
        gives[-1].start()
    for cp in gives:
        cp.wait()


def finish(cg, fg, factor):
    parts = 8
    hbm = pl.BlockSpec(memory_space=pl.ANY)
    return pl.pallas_call(
        functools.partial(finish_kernel, factor),
        out_shape=(
            jax.ShapeDtypeStruct(cg.shape, F32),
            jax.ShapeDtypeStruct(fg.shape, BF),
        ),
        in_specs=[pl.BlockSpec(memory_space=pltpu.VMEM)] * 2,
        out_specs=(hbm, hbm),
        scratch_shapes=[
            pltpu.VMEM((parts, CODES // parts, HD), F32),
            pltpu.SemaphoreType.DMA((parts + 1,)),
        ],
        compiler_params=pltpu.CompilerParams(vmem_limit_bytes=40 << 20),
        name="widen",
    )(cg, fg)


def on_device(features, conv_weight, codebook, recon_grad):
    dma = pltpu.SemaphoreType.DMA
    vm = pltpu.VMEM
    hbm = pl.BlockSpec(memory_space=pl.ANY)
    sems = [12, 2, 2, 2, 2, 8, 8, 7, 7, 7, 7, 4, 4, 4, 4, 4, 4, 16, 16, 7, 7, 7, 7, 3, 3, 8, 2]
    cg, fg = pl.pallas_call(
        kernel,
        out_shape=(
            pltpu.VMEM((CODES, HD), BF),
            pltpu.VMEM((IMG, BAND, LW, CIN), BF),
        ),
        in_specs=[hbm] * 4,
        out_specs=(pl.BlockSpec(memory_space=pltpu.VMEM), pl.BlockSpec(memory_space=pltpu.VMEM)),
        scratch_shapes=[
            vm((BAND + 2, IMG, LW, CIN), BF),
            vm((3, 3, CIN, D), BF),
            vm((HALF, D), F32),
            vm((HALF, D), BF),
            vm((HALF, D), BF),
            vm((4 * ROWS // LW, LW, D), BF),
            vm((2 * ROWS // LW, LW, D), BF),
            vm((HALF, 2 * ROWS), F32),
            vm((HALF, 2 * ROWS), F32),
            vm((NX, 1, 2 * ROWS), F32),
            vm((PART, 4 * ROWS), BF),
            vm((HALF, 2 * ROWS), BF),
            vm((HALF, 2 * ROWS), BF),
            vm((D, 2 * ROWS), F32),
            vm((D, 2 * ROWS), F32),
            vm((8, 128), F32),
            vm((7, 8, 128), F32),
            vm((NZ, 8, 128), F32),
            vm((4, QTR, D), BF),
            vm((4, PART, D), BF),
            vm((4, QTR, D), F32),
            vm((4, QTR, D), BF),
            vm((2, PART, D), BF),
            vm((2, PART, D), BF),
            vm((2, PART, D), F32),
            vm((2, 2, PART, HD), BF),
            vm((D, HALF), BF),
            vm((2 * ROWS, D), BF),
            vm((7, OWN, D), BF),
            vm((OWN, D), BF),
            vm((NZ - 1, OWN, D), BF),
            vm((OWN, D), BF),
            vm((BAND + 2, OWN, D), BF),
        ] + [dma((n,)) for n in sems] + [pltpu.SemaphoreType.REGULAR((2,))],
        compiler_params=pltpu.CompilerParams(
            collective_id=0, has_side_effects=True, vmem_limit_bytes=58 << 20
        ),
        cost_estimate=pl.CostEstimate(
            flops=12 * 2**30, bytes_accessed=10 << 20, transcendentals=1 << 21
        ),
        name="soft_quantize",
    )(features, conv_weight, codebook, recon_grad)
    entries_all = codebook.shape[0] * lax.axis_size("code")
    rows_all = ROWS * lax.axis_size("dp") * lax.axis_size("spatial")
    return finish(cg, fg, entries_all / rows_all)


def solution(mesh):
    placed = (P("dp", "spatial", None, None), P(), P("code", None), P("dp", "spatial", None, None))
    return jax.shard_map(
        on_device,
        mesh=mesh,
        in_specs=placed,
        out_specs=(P("code", "dp"), P("dp", "spatial", None, None)),
        check_vma=False,
    )
```

```python
import functools

import jax
import jax.numpy as jnp
from jax import lax
from jax.experimental import pallas as pl
from jax.experimental.pallas import tpu as pltpu
from jax.sharding import PartitionSpec as P

MESH = pl.DeviceIdType.MESH
BF = jnp.bfloat16
F32 = jnp.float32
NX, NY, NZ = 4, 4, 8
IMG, BAND, LW, CIN, D = 4, 4, 16, 512, 256
ROWS = IMG * BAND * LW
CODES = 4096
HALF = CODES // 2
BLK = HALF // NX
PART = BLK // 2
QTR = PART // 2
OWN = IMG * LW
UNIT = OWN // LW
HD = D // 2


def nt(a, b):
    return lax.dot_general(a, b, (((1,), (1,)), ((), ())), preferred_element_type=F32)


def nn(a, b):
    return lax.dot_general(a, b, (((1,), (0,)), ((), ())), preferred_element_type=F32)


def tn(a, b):
    return lax.dot_general(a, b, (((0,), (0,)), ((), ())), preferred_element_type=F32)


def shifted(acc, step):
    rows = acc.shape[0]
    col = lax.broadcasted_iota(jnp.int32, acc.shape, 0) % LW
    keep = (col >= 1) if step == 1 else (col < LW - 1)
    return jnp.where(keep, pltpu.roll(acc, step % rows, 0), 0.0)


def kernel(
    feat, cw_hbm, cb_hbm, up,
    cg, fg,
    xp, cw, cb, hi, lo, right, lat_lo, wts, proj, mst, pg, wb, gb, sum_w, sum_g,
    st, st_col, st_z, far, near, mid, got_far, got_left, got_right, own, fin,
    hi_t, gsum, g_col, gz_src, g_z, lg_src, lg,
    l_sem, h_ss, h_rs, u_ss, u_rs, t_ss, t_rs, sc_ss, sc_rs, sz_ss, sz_rs,
    r2_ss, r2_rs, rd_ss, rd_rs, rm_ss, rm_rs, a_ss, a_rs, gc_ss, gc_rs, gz_ss, gz_rs, lg_ss, lg_rs, e_ss, e_rs, z_sem,
):
    d, s, k = lax.axis_index("dp"), lax.axis_index("spatial"), lax.axis_index("code")
    z, yh, c = k // 4, (k // 2) % 2, k % 2
    y = yh * 2 + d

    def dev(x_, y_, z_, c_):
        return (y_ % 2, x_, z_ * 4 + (y_ // 2) * 2 + c_)

    def xdev(o):
        return dev((s + o) % NX, y, z, c)

    def ydev(j):
        return dev(s, (y + j) % NY, z, c)

    def coldev(i):
        return dev(s, (y + i // 2) % NY, z, (c + i) % 2)

    def zdev(i):
        return dev(s, y, (z + i) % NZ, c)

    def agdev(f, o):
        return ((d + f) % 2, (s + o) % NX, k)

    def edgedev(e, i):
        return dev((s + e) % NX, (y + 2 * (i // 2)) % NY, z, (c + i) % 2)

    def remote(src, dst, ss, rs, who):
        return pltpu.make_async_remote_copy(
            src_ref=src, dst_ref=dst, send_sem=ss, recv_sem=rs,
            device_id=who, device_id_type=MESH,
        )

    load_cb = pltpu.make_async_copy(cb_hbm.at[pl.ds(d * HALF, HALF)], cb, l_sem.at[0])
    load_u = [
        pltpu.make_async_copy(up.at[:, h], right.at[pl.ds(h * UNIT, UNIT)], l_sem.at[4 + h])
        for h in range(BAND)
    ]
    load_x = [
        pltpu.make_async_copy(feat.at[:, h], xp.at[1 + h], l_sem.at[8 + h]) for h in range(BAND)
    ]
    load_w = pltpu.make_async_copy(cw_hbm, cw, l_sem.at[1])
    barrier = pltpu.get_barrier_semaphore()
    peers = [xdev(1), xdev(NX - 1), ydev(1), ydev(NY - 1), zdev(1), zdev(NZ - 1)]
    peers.append(dev(s, y, z, 1 - c))
    for who in peers:
        pl.semaphore_signal(barrier, inc=1, device_id=who, device_id_type=MESH)
    load_cb.start()
    for cp in load_x + [load_w] + load_u:
        cp.start()
    load_cb.wait()

    @pl.loop(0, HALF // 256)
    def _(i):
        rows = pl.ds(pl.multiple_of(i * 256, 256), 256)
        v = cb[rows, :]
        h = v.astype(BF)
        hi[rows, :] = h
        lo[rows, :] = (v - h.astype(F32)).astype(BF)

    pl.semaphore_wait(barrier, len(peers))

    for cp in load_u:
        cp.wait()
    halo = [
        remote(feat.at[:, BAND - 1], xp.at[0], h_ss.at[0], h_rs.at[0], xdev(1)),
        remote(feat.at[:, 0], xp.at[BAND + 1], h_ss.at[1], h_rs.at[1], xdev(NX - 1)),
    ]
    sides = (1, NY - 1)

    def share(buf, at, count, peer_at, ss, rs, n):
        return remote(
            buf.at[pl.ds(at, count)], buf.at[pl.ds(peer_at, count)], ss.at[n], rs.at[n], ydev(sides[n % 2])
        )

    quarter = ROWS // LW
    give_u = [
        share(right, n * 2 * UNIT, 2 * UNIT, quarter + n * 2 * UNIT, u_ss, u_rs, n) for n in range(2)
    ]
    for cp in halo + give_u:
        cp.start()

    def tell(n, reach):
        for i in (reach, NZ - reach):
            pl.semaphore_signal(z_sem.at[n], inc=1, device_id=zdev(i), device_id_type=MESH)

    tell(0, 1)

    def rows_of(buf, n):
        return buf[n * quarter:(n + 1) * quarter].reshape(ROWS, D)

    def project(rb):
        u = rows_of(right, rb)
        for i in range(NX):
            rows = slice(i * BLK, (i + 1) * BLK)
            proj[rows, rb * ROWS:(rb + 1) * ROWS] = nt(hi[rows, :], u) + nt(lo[rows, :], u)

    give_t = []

    def convolve(grid_rows):
        def taps(b):
            acc = None
            for a in range(3):
                xa = jnp.concatenate([xp[h + a].reshape(OWN, CIN) for h in grid_rows], axis=0)
                t = nn(xa, cw[a, b])
                acc = t if acc is None else acc + t
            return acc

        latent = taps(1) + shifted(taps(0), 1) + shifted(taps(2), -1)
        lat_hi = latent.astype(BF)
        rest = (latent - lat_hi.astype(F32)).astype(BF)
        for n, h in enumerate(grid_rows):
            at = slice(n * OWN, (n + 1) * OWN)
            right[2 * quarter + h * UNIT:2 * quarter + (h + 1) * UNIT] = lat_hi[at].reshape(UNIT, LW, D)
            lat_lo[h * UNIT:(h + 1) * UNIT] = rest[at].reshape(UNIT, LW, D)
        for n, h in enumerate(grid_rows):
            m = len(give_t)
            give_t.append(share(right, 2 * quarter + h * UNIT, UNIT, 3 * quarter + h * UNIT, t_ss, t_rs, m))
            give_t[-1].start()
        for n, h in enumerate(grid_rows):
            m = len(give_t)
            give_t.append(share(lat_lo, h * UNIT, UNIT, quarter + h * UNIT, t_ss, t_rs, m))
            give_t[-1].start()

    for cp in load_x + [load_w]:
        cp.wait()
    convolve((1, 2))
    project(0)

    @pl.loop(0, HALF // 256)
    def _(i):
        at = pl.ds(pl.multiple_of(i * 256, 256), 256)
        hi_t[:, at] = hi[at, :].T

    pl.semaphore_wait(z_sem.at[0], 2)
    tell(1, 2)
    for cp in halo + give_u:
        cp.wait_recv()

    @pl.when(s == 0)
    def _():
        xp[0] = jnp.zeros((IMG, LW, CIN), BF)

    @pl.when(s == NX - 1)
    def _():
        xp[BAND + 1] = jnp.zeros((IMG, LW, CIN), BF)

    convolve((0, BAND - 1))

    def merge(a, b):
        top = jnp.maximum(a[0], b[0])
        ea, eb = jnp.exp(a[0] - top), jnp.exp(b[0] - top)
        return top, a[1] * ea + b[1] * eb, a[2] * ea + b[2] * eb

    def score(rb):
        cols = slice(rb * ROWS, (rb + 1) * ROWS)
        lh = rows_of(right, 2 + rb)
        ll = rows_of(lat_lo, rb)

        def step(i, carry):
            rows = slice(i * BLK, (i + 1) * BLK)
            h = hi[rows, :]
            sc = nt(h, lh) + (nt(h, ll) + nt(lo[rows, :], lh))
            top = jnp.max(sc, axis=0, keepdims=True)
            w = jnp.exp(sc - top)
            wts[rows, cols] = w
            mst[i, :, cols] = top
            mass = jnp.sum(w, axis=0, keepdims=True)
            dots = jnp.sum(w * proj[rows, cols], axis=0, keepdims=True)
            return merge(carry, (top, mass, dots))

        zero = jnp.zeros((1, ROWS), F32)
        carry = (zero - 3.0e38, zero, zero)
        for i in range(NX):
            carry = step(i, carry)
        top, mass, dots = carry
        logs, mean = top + jnp.log(mass), dots / mass
        for n in range(2):
            st[2 * rb + n:2 * rb + n + 1, :] = logs[:, n * 128:(n + 1) * 128]
            st[4 + 2 * rb + n:5 + 2 * rb + n, :] = mean[:, n * 128:(n + 1) * 128]
        return logs, mean

    ends = [score(0)]
    pl.semaphore_wait(z_sem.at[1], 2)
    project(1)
    for cp in give_t:
        cp.wait_recv()
    ends.append(score(1))

    def combine(parts):
        top = functools.reduce(jnp.maximum, [p[:4] for p in parts])
        mass, dots = 0.0, 0.0
        for p in parts:
            e = jnp.exp(p[:4] - top)
            mass, dots = mass + e, dots + e * p[4:]
        return top + jnp.log(mass), dots / mass

    def swap(p):
        return jnp.concatenate([p[2:4], p[0:2], p[6:8], p[4:6]], axis=0)

    col = [remote(st, st_col.at[i - 1], sc_ss.at[i - 1], sc_rs.at[i - 1], coldev(i)) for i in range(1, 8)]
    for cp in col:
        cp.start()

    own_logs = jnp.concatenate([e[0] for e in ends], axis=1)
    own_mean = jnp.concatenate([e[1] for e in ends], axis=1)
    for i in range(2 * NX):
        rows = slice(i * PART, (i + 1) * PART)
        w = wts[rows, :] * jnp.exp(mst[i // 2] - own_logs)
        wb[rows, :] = w.astype(BF)
        gb[rows, :] = (w * (proj[rows, :] - own_mean)).astype(BF)
    sum_g[...] = nn(hi_t[...], gb[...])
    sum_w[...] = nn(hi_t[...], wb[...])

    for cp in col:
        cp.wait_recv()
    parts = [st[...]]
    for i in range(1, 8):
        p = st_col[i - 1]
        parts.append(swap(p) if (i // 2) % 2 else p)
    logs, mean = combine(parts)
    st_z[0] = jnp.concatenate([logs, mean], axis=0)
    zs = [remote(st_z.at[0], st_z.at[i], sz_ss.at[i - 1], sz_rs.at[i - 1], zdev(i)) for i in range(1, NZ)]
    for cp in zs:
        cp.start()
    for cp in zs:
        cp.wait_recv()
    logs, mean = combine([st_z[i] for i in range(NZ)])
    total = jnp.concatenate([logs[n:n + 1] for n in range(4)], axis=1)
    inner = jnp.concatenate([mean[n:n + 1] for n in range(4)], axis=1)

    both = 2 * ROWS

    def term(o, h):
        blk = (s + o) % NX
        rows = pl.ds(pl.multiple_of(blk * BLK + h * PART, PART), PART)
        p = wts[rows, :] * jnp.exp(mst[blk] - total)
        g = (p * (proj[rows, :] - inner)).astype(BF)
        pg[:, :both] = p.astype(BF)
        pg[:, both:] = g
        return nn(pg[...], right[...].reshape(4 * ROWS, D))

    def grid_row(y_, c_):
        return (y_ // 2) * 2 + c_

    gcol = []
    for i in range(1, 8):
        j = i // 2
        base = (j % 2) * ROWS + grid_row((y + j) % NY, (c + i) % 2) * OWN
        rows = pl.ds(pl.multiple_of(base, OWN), OWN)
        gcol.append(remote(gsum.at[rows], g_col.at[i - 1], gc_ss.at[i - 1], gc_rs.at[i - 1], coldev(i)))

    near_x = (1, NX - 1)
    first, second = slice(0, QTR), slice(QTR, PART)
    ring, direct, summed = [], [], []

    def send_far(h):
        t = term(2, h).astype(BF)
        for n, half in enumerate((first, second)):
            m = 2 * h + n
            far[m] = t[half]
            cp = remote(far.at[m], got_far.at[m], r2_ss.at[m], r2_rs.at[m], xdev(near_x[n]))
            cp.start()
            ring.append(cp)

    def send_near(h):
        for n, (now, later) in enumerate(((second, first), (first, second))):
            m = 2 * h + n
            t = term(near_x[n], h)
            mid[m] = t[later]
            near[m, now] = t[now].astype(BF)
            at = pl.ds(now.start, QTR)
            to = (got_left, got_right)[n]
            cp = remote(near.at[m, at], to.at[h, at], rd_ss.at[m], rd_rs.at[m], xdev(near_x[n]))
            cp.start()
            direct.append(cp)

    def send_sum(h):
        for n, later in enumerate((first, second)):
            m = 2 * h + n
            ring[m].wait_recv()
            near[m, later] = (mid[m] + got_far[m].astype(F32)).astype(BF)
            at = pl.ds(later.start, QTR)
            to = (got_left, got_right)[n]
            cp = remote(near.at[m, at], to.at[h, at], rm_ss.at[m], rm_rs.at[m], xdev(near_x[n]))
            cp.start()
            summed.append(cp)

    send_far(0)
    send_near(0)
    send_far(1)
    share_of = jnp.exp(own_logs - total)
    gsum[...] = (share_of * (sum_g[...] + (own_mean - inner) * sum_w[...])).T.astype(BF)
    for cp in gcol:
        cp.start()
    own[0] = term(0, 0)
    send_sum(0)
    send_near(1)
    own[1] = term(0, 1)
    send_sum(1)

    for cp in gcol:
        cp.wait_recv()
    mine = grid_row(y, c)
    part = gsum[pl.ds(pl.multiple_of(mine * OWN, OWN), OWN), :].astype(F32)
    for i in range(7):
        part = part + g_col[i].astype(F32)
    gz_src[...] = part.astype(BF)
    gzs = [remote(gz_src, g_z.at[i - 1], gz_ss.at[i - 1], gz_rs.at[i - 1], zdev(i)) for i in range(1, NZ)]
    for cp in gzs:
        cp.start()

    out, over, keep = [], [], []

    def spread(h):
        for n in range(2):
            direct[2 * h + n].wait_recv()
            summed[2 * h + n].wait_recv()
        block = own[h] + got_left[h].astype(F32) + got_right[h].astype(F32)
        left, rest = block[:, :HD].astype(BF), block[:, HD:].astype(BF)
        fin[h, 0] = jnp.where(d == 0, left, rest)
        fin[h, 1] = jnp.where(d == 0, rest, left)
        place = cg.at[pl.ds(pl.multiple_of(d * HALF + s * BLK + h * PART, PART), PART)]
        n = 8 * h + NX
        over.append(remote(fin.at[h, 1], place, a_ss.at[n], a_rs.at[n], agdev(1, 0)))
        over[-1].start()
        for o in (2, 1, 3):
            n = 8 * h + o
            out.append(remote(fin.at[h, 0], place, a_ss.at[n], a_rs.at[n], agdev(0, o)))
            out[-1].start()
        keep.append(pltpu.make_async_copy(fin.at[h, 0], place, l_sem.at[2 + h]))
        keep[-1].start()

    def relay(h):
        over[h].wait_recv()
        place = cg.at[pl.ds(pl.multiple_of((1 - d) * HALF + s * BLK + h * PART, PART), PART)]
        for o in (2, 1, 3):
            n = 8 * h + NX + o
            out.append(remote(place, place, a_ss.at[n], a_rs.at[n], agdev(0, o)))
            out[-1].start()

    spread(0)
    spread(1)
    relay(0)

    for cp in gzs:
        cp.wait_recv()
    for i in range(NZ - 1):
        part = part + g_z[i].astype(F32)
    lg_src[...] = part.astype(BF)
    lg[1 + mine] = lg_src[...]
    back = [
        remote(lg_src, lg.at[1 + mine], lg_ss.at[n], lg_rs.at[n], coldev(i))
        for n, i in enumerate((1, 4, 5))
    ]
    edges = []
    for n, (e, to) in enumerate(((1, 0), (NX - 1, BAND + 1))):
        edges.append([
            remote(lg_src, lg.at[to], e_ss.at[n * 4 + i], e_rs.at[n], edgedev(e, i)) for i in range(4)
        ])
    edge_row = (BAND - 1, 0)
    for n in range(2):

        @pl.when(mine == edge_row[n])
        def _():
            for cp in edges[n]:
                cp.start()

    for cp in back:
        cp.start()
    relay(1)
    for cp in back + [edges[0][0], edges[1][0]]:
        cp.wait_recv()

    @pl.when(s == 0)
    def _():
        lg[0] = jnp.zeros((OWN, D), BF)

    @pl.when(s == NX - 1)
    def _():
        lg[BAND + 1] = jnp.zeros((OWN, D), BF)

    def back_taps(b):
        acc = None
        for a in range(3):
            la = lg[2 - a:2 - a + BAND].reshape(ROWS, D)
            t = nt(la, cw[a, b])
            acc = t if acc is None else acc + t
        return acc

    grad = back_taps(1) + shifted(back_taps(0), -1) + shifted(back_taps(2), 1)
    for h in range(BAND):
        fg[:, h] = grad[h * OWN:(h + 1) * OWN].astype(BF).reshape(IMG, LW, CIN)
    for n in range(2):

        @pl.when(mine == edge_row[n])
        def _():
            for cp in edges[n]:
                cp.wait_send()

    for cp in halo + give_u + give_t + col + zs + ring + direct + summed + gcol + gzs + back + over:
        cp.wait_send()
    for cp in keep + out:
        cp.wait()


def finish_kernel(factor, cg, fg, out_cg, out_fg, wide, sem):
    parts = wide.shape[0]
    rows = CODES // parts
    gives = [pltpu.make_async_copy(fg, out_fg, sem.at[parts])]
    gives[0].start()
    for n in range(parts):
        at = pl.ds(n * rows, rows)
        wide[n] = cg[at, :].astype(F32) * factor
        gives.append(pltpu.make_async_copy(wide.at[n], out_cg.at[at], sem.at[n]))
        gives[-1].start()
    for cp in gives:
        cp.wait()


def finish(cg, fg, factor):
    parts = 8
    hbm = pl.BlockSpec(memory_space=pl.ANY)
    return pl.pallas_call(
        functools.partial(finish_kernel, factor),
        out_shape=(
            jax.ShapeDtypeStruct(cg.shape, F32),
            jax.ShapeDtypeStruct(fg.shape, BF),
        ),
        in_specs=[pl.BlockSpec(memory_space=pltpu.VMEM)] * 2,
        out_specs=(hbm, hbm),
        scratch_shapes=[
            pltpu.VMEM((parts, CODES // parts, HD), F32),
            pltpu.SemaphoreType.DMA((parts + 1,)),
        ],
        compiler_params=pltpu.CompilerParams(vmem_limit_bytes=40 << 20),
        name="widen",
    )(cg, fg)


def on_device(features, conv_weight, codebook, recon_grad):
    dma = pltpu.SemaphoreType.DMA
    vm = pltpu.VMEM
    hbm = pl.BlockSpec(memory_space=pl.ANY)
    sems = [12, 2, 2, 2, 2, 8, 8, 7, 7, 7, 7, 4, 4, 4, 4, 4, 4, 16, 16, 7, 7, 7, 7, 3, 3, 8, 2]
    cg, fg = pl.pallas_call(
        kernel,
        out_shape=(
            pltpu.VMEM((CODES, HD), BF),
            pltpu.VMEM((IMG, BAND, LW, CIN), BF),
        ),
        in_specs=[hbm] * 4,
        out_specs=(pl.BlockSpec(memory_space=pltpu.VMEM), pl.BlockSpec(memory_space=pltpu.VMEM)),
        scratch_shapes=[
            vm((BAND + 2, IMG, LW, CIN), BF),
            vm((3, 3, CIN, D), BF),
            vm((HALF, D), F32),
            vm((HALF, D), BF),
            vm((HALF, D), BF),
            vm((4 * ROWS // LW, LW, D), BF),
            vm((2 * ROWS // LW, LW, D), BF),
            vm((HALF, 2 * ROWS), F32),
            vm((HALF, 2 * ROWS), F32),
            vm((NX, 1, 2 * ROWS), F32),
            vm((PART, 4 * ROWS), BF),
            vm((HALF, 2 * ROWS), BF),
            vm((HALF, 2 * ROWS), BF),
            vm((D, 2 * ROWS), F32),
            vm((D, 2 * ROWS), F32),
            vm((8, 128), F32),
            vm((7, 8, 128), F32),
            vm((NZ, 8, 128), F32),
            vm((4, QTR, D), BF),
            vm((4, PART, D), BF),
            vm((4, QTR, D), F32),
            vm((4, QTR, D), BF),
            vm((2, PART, D), BF),
            vm((2, PART, D), BF),
            vm((2, PART, D), F32),
            vm((2, 2, PART, HD), BF),
            vm((D, HALF), BF),
            vm((2 * ROWS, D), BF),
            vm((7, OWN, D), BF),
            vm((OWN, D), BF),
            vm((NZ - 1, OWN, D), BF),
            vm((OWN, D), BF),
            vm((BAND + 2, OWN, D), BF),
        ] + [dma((n,)) for n in sems] + [pltpu.SemaphoreType.REGULAR((2,))],
        compiler_params=pltpu.CompilerParams(
            collective_id=0, has_side_effects=True, vmem_limit_bytes=58 << 20
        ),
        cost_estimate=pl.CostEstimate(
            flops=12 * 2**30, bytes_accessed=10 << 20, transcendentals=1 << 21
        ),
        name="soft_quantize",
    )(features, conv_weight, codebook, recon_grad)
    entries_all = codebook.shape[0] * lax.axis_size("code")
    rows_all = ROWS * lax.axis_size("dp") * lax.axis_size("spatial")
    return finish(cg, fg, entries_all / rows_all)


def solution(mesh):
    placed = (P("dp", "spatial", None, None), P(), P("code", None), P("dp", "spatial", None, None))
    return jax.shard_map(
        on_device,
        mesh=mesh,
        in_specs=placed,
        out_specs=(P("code", "dp"), P("dp", "spatial", None, None)),
        check_vma=False,
    )
```

```python
import functools

import jax
import jax.numpy as jnp
from jax import lax
from jax.experimental import pallas as pl
from jax.experimental.pallas import tpu as pltpu
from jax.sharding import PartitionSpec as P

MESH = pl.DeviceIdType.MESH
BF = jnp.bfloat16
F32 = jnp.float32
NX, NY, NZ = 4, 4, 8
IMG, BAND, LW, CIN, D = 4, 4, 16, 512, 256
ROWS = IMG * BAND * LW
CODES = 4096
HALF = CODES // 2
BLK = HALF // NX
PART = BLK // 2
QTR = PART // 2
OWN = IMG * LW
UNIT = OWN // LW
HD = D // 2
COL_ORDER = (5, 4, 3, 7, 2, 6, 1)
Z_ORDER = (4, 3, 5, 2, 6, 1, 7)


def nt(a, b):
    return lax.dot_general(a, b, (((1,), (1,)), ((), ())), preferred_element_type=F32)


def nn(a, b):
    return lax.dot_general(a, b, (((1,), (0,)), ((), ())), preferred_element_type=F32)


def tn(a, b):
    return lax.dot_general(a, b, (((0,), (0,)), ((), ())), preferred_element_type=F32)


def shifted(acc, step):
    rows = acc.shape[0]
    col = lax.broadcasted_iota(jnp.int32, acc.shape, 0) % LW
    keep = (col >= 1) if step == 1 else (col < LW - 1)
    return jnp.where(keep, pltpu.roll(acc, step % rows, 0), 0.0)


def kernel(
    feat, cw_hbm, cb_hbm, up,
    cg, fg,
    xp, cw, cb, hi, lo, right, lat_lo, wts, proj, mst, pg, wb, gb, sum_w, sum_g,
    st, st_col, st_z, far, near, mid, got_far, got_left, got_right, own, fin,
    hi_t, gsum, g_col, gz_src, g_z, lg_src, lg,
    l_sem, h_ss, h_rs, u_ss, u_rs, t_ss, t_rs, sc_ss, sc_rs, sz_ss, sz_rs,
    r2_ss, r2_rs, rd_ss, rd_rs, rm_ss, rm_rs, a_ss, a_rs, gc_ss, gc_rs, gz_ss, gz_rs, lg_ss, lg_rs, e_ss, e_rs, z_sem,
):
    d, s, k = lax.axis_index("dp"), lax.axis_index("spatial"), lax.axis_index("code")
    z, yh, c = k // 4, (k // 2) % 2, k % 2
    y = yh * 2 + d

    def dev(x_, y_, z_, c_):
        return (y_ % 2, x_, z_ * 4 + (y_ // 2) * 2 + c_)

    def xdev(o):
        return dev((s + o) % NX, y, z, c)

    def ydev(j):
        return dev(s, (y + j) % NY, z, c)

    def coldev(i):
        return dev(s, (y + i // 2) % NY, z, (c + i) % 2)

    def zdev(i):
        return dev(s, y, (z + i) % NZ, c)

    def agdev(f, o):
        return ((d + f) % 2, (s + o) % NX, k)

    def edgedev(e, i):
        return dev((s + e) % NX, (y + 2 * (i // 2)) % NY, z, (c + i) % 2)

    def remote(src, dst, ss, rs, who):
        return pltpu.make_async_remote_copy(
            src_ref=src, dst_ref=dst, send_sem=ss, recv_sem=rs,
            device_id=who, device_id_type=MESH,
        )

    load_cb = pltpu.make_async_copy(cb_hbm.at[pl.ds(d * HALF, HALF)], cb, l_sem.at[0])
    load_u = [
        pltpu.make_async_copy(up.at[:, h], right.at[pl.ds(h * UNIT, UNIT)], l_sem.at[4 + h])
        for h in range(BAND)
    ]
    load_x = [
        pltpu.make_async_copy(feat.at[:, h], xp.at[1 + h], l_sem.at[8 + h]) for h in range(BAND)
    ]
    load_w = pltpu.make_async_copy(cw_hbm, cw, l_sem.at[1])
    barrier = pltpu.get_barrier_semaphore()
    peers = [xdev(1), xdev(NX - 1), ydev(1), ydev(NY - 1), zdev(1), zdev(NZ - 1)]
    peers.append(dev(s, y, z, 1 - c))
    for who in peers:
        pl.semaphore_signal(barrier, inc=1, device_id=who, device_id_type=MESH)
    for cp in load_u + load_x + [load_w, load_cb]:
        cp.start()
    pl.semaphore_wait(barrier, len(peers))

    halo = [
        remote(feat.at[:, BAND - 1], xp.at[0], h_ss.at[0], h_rs.at[0], xdev(1)),
        remote(feat.at[:, 0], xp.at[BAND + 1], h_ss.at[1], h_rs.at[1], xdev(NX - 1)),
    ]
    sides = (1, NY - 1)

    def share(buf, at, count, peer_at, ss, rs, n):
        return remote(
            buf.at[pl.ds(at, count)], buf.at[pl.ds(peer_at, count)], ss.at[n], rs.at[n], ydev(sides[n % 2])
        )

    quarter = ROWS // LW
    give_u = [
        share(right, n * 2 * UNIT, 2 * UNIT, quarter + n * 2 * UNIT, u_ss, u_rs, n) for n in range(2)
    ]
    for cp in halo:
        cp.start()
    for cp in load_u:
        cp.wait()
    for cp in give_u:
        cp.start()

    def tell(n, reach):
        for i in (reach, NZ - reach):
            pl.semaphore_signal(z_sem.at[n], inc=1, device_id=zdev(i), device_id_type=MESH)

    tell(0, 1)

    def rows_of(buf, n):
        return buf[n * quarter:(n + 1) * quarter].reshape(ROWS, D)

    def project(rb):
        u = rows_of(right, rb)
        for i in range(NX):
            rows = slice(i * BLK, (i + 1) * BLK)
            proj[rows, rb * ROWS:(rb + 1) * ROWS] = nt(hi[rows, :], u) + nt(lo[rows, :], u)

    give_t = []

    def convolve(grid_rows):
        def taps(b):
            acc = None
            for a in range(3):
                xa = jnp.concatenate([xp[h + a].reshape(OWN, CIN) for h in grid_rows], axis=0)
                t = nn(xa, cw[a, b])
                acc = t if acc is None else acc + t
            return acc

        latent = taps(1) + shifted(taps(0), 1) + shifted(taps(2), -1)
        lat_hi = latent.astype(BF)
        rest = (latent - lat_hi.astype(F32)).astype(BF)
        for n, h in enumerate(grid_rows):
            at = slice(n * OWN, (n + 1) * OWN)
            right[2 * quarter + h * UNIT:2 * quarter + (h + 1) * UNIT] = lat_hi[at].reshape(UNIT, LW, D)
            lat_lo[h * UNIT:(h + 1) * UNIT] = rest[at].reshape(UNIT, LW, D)
        for n, h in enumerate(grid_rows):
            m = len(give_t)
            give_t.append(share(right, 2 * quarter + h * UNIT, UNIT, 3 * quarter + h * UNIT, t_ss, t_rs, m))
            give_t[-1].start()
        for n, h in enumerate(grid_rows):
            m = len(give_t)
            give_t.append(share(lat_lo, h * UNIT, UNIT, quarter + h * UNIT, t_ss, t_rs, m))
            give_t[-1].start()

    for cp in load_x + [load_w]:
        cp.wait()
    convolve((1, 2))
    load_cb.wait()

    @pl.loop(0, HALF // 256)
    def _(i):
        rows = pl.ds(pl.multiple_of(i * 256, 256), 256)
        v = cb[rows, :]
        h = v.astype(BF)
        hi[rows, :] = h
        lo[rows, :] = (v - h.astype(F32)).astype(BF)

    project(0)

    pl.semaphore_wait(z_sem.at[0], 2)
    tell(1, 2)
    for cp in halo + give_u:
        cp.wait_recv()

    @pl.when(s == 0)
    def _():
        xp[0] = jnp.zeros((IMG, LW, CIN), BF)

    @pl.when(s == NX - 1)
    def _():
        xp[BAND + 1] = jnp.zeros((IMG, LW, CIN), BF)

    convolve((0, BAND - 1))

    def merge(a, b):
        top = jnp.maximum(a[0], b[0])
        ea, eb = jnp.exp(a[0] - top), jnp.exp(b[0] - top)
        return top, a[1] * ea + b[1] * eb, a[2] * ea + b[2] * eb

    def score(rb):
        cols = slice(rb * ROWS, (rb + 1) * ROWS)
        lh = rows_of(right, 2 + rb)
        ll = rows_of(lat_lo, rb)

        def step(i, carry):
            rows = slice(i * BLK, (i + 1) * BLK)
            h = hi[rows, :]
            sc = nt(h, lh) + (nt(h, ll) + nt(lo[rows, :], lh))
            top = jnp.max(sc, axis=0, keepdims=True)
            w = jnp.exp(sc - top)
            wts[rows, cols] = w
            mst[i, :, cols] = top
            mass = jnp.sum(w, axis=0, keepdims=True)
            dots = jnp.sum(w * proj[rows, cols], axis=0, keepdims=True)
            return merge(carry, (top, mass, dots))

        zero = jnp.zeros((1, ROWS), F32)
        carry = (zero - 3.0e38, zero, zero)
        for i in range(NX):
            carry = step(i, carry)
        top, mass, dots = carry
        logs, mean = top + jnp.log(mass), dots / mass
        for n in range(2):
            st[2 * rb + n:2 * rb + n + 1, :] = logs[:, n * 128:(n + 1) * 128]
            st[4 + 2 * rb + n:5 + 2 * rb + n, :] = mean[:, n * 128:(n + 1) * 128]
        return logs, mean

    ends = [score(0)]
    pl.semaphore_wait(z_sem.at[1], 2)
    project(1)
    for cp in give_t:
        cp.wait_recv()
    ends.append(score(1))

    def combine(parts):
        top = functools.reduce(jnp.maximum, [p[:4] for p in parts])
        mass, dots = 0.0, 0.0
        for p in parts:
            e = jnp.exp(p[:4] - top)
            mass, dots = mass + e, dots + e * p[4:]
        return top + jnp.log(mass), dots / mass

    def swap(p):
        return jnp.concatenate([p[2:4], p[0:2], p[6:8], p[4:6]], axis=0)

    col = [remote(st, st_col.at[i - 1], sc_ss.at[i - 1], sc_rs.at[i - 1], coldev(i)) for i in range(1, 8)]
    for i in COL_ORDER:
        col[i - 1].start()

    @pl.loop(0, HALF // 256)
    def _(i):
        at = pl.ds(pl.multiple_of(i * 256, 256), 256)
        hi_t[:, at] = hi[at, :].T

    own_logs = jnp.concatenate([e[0] for e in ends], axis=1)
    own_mean = jnp.concatenate([e[1] for e in ends], axis=1)
    for i in range(2 * NX):
        rows = slice(i * PART, (i + 1) * PART)
        w = wts[rows, :] * jnp.exp(mst[i // 2] - own_logs)
        wb[rows, :] = w.astype(BF)
        gb[rows, :] = (w * (proj[rows, :] - own_mean)).astype(BF)
    sum_g[...] = nn(hi_t[...], gb[...])

    for cp in col:
        cp.wait_recv()
    parts = [st[...]]
    for i in range(1, 8):
        p = st_col[i - 1]
        parts.append(swap(p) if (i // 2) % 2 else p)
    logs, mean = combine(parts)
    st_z[0] = jnp.concatenate([logs, mean], axis=0)
    zs = [remote(st_z.at[0], st_z.at[i], sz_ss.at[i - 1], sz_rs.at[i - 1], zdev(i)) for i in range(1, NZ)]
    for i in Z_ORDER:
        zs[i - 1].start()
    sum_w[...] = nn(hi_t[...], wb[...])
    for cp in zs:
        cp.wait_recv()
    logs, mean = combine([st_z[i] for i in range(NZ)])
    total = jnp.concatenate([logs[n:n + 1] for n in range(4)], axis=1)
    inner = jnp.concatenate([mean[n:n + 1] for n in range(4)], axis=1)

    both = 2 * ROWS

    def term(o, h):
        blk = (s + o) % NX
        rows = pl.ds(pl.multiple_of(blk * BLK + h * PART, PART), PART)
        p = wts[rows, :] * jnp.exp(mst[blk] - total)
        g = (p * (proj[rows, :] - inner)).astype(BF)
        pg[:, :both] = p.astype(BF)
        pg[:, both:] = g
        return nn(pg[...], right[...].reshape(4 * ROWS, D))

    def grid_row(y_, c_):
        return (y_ // 2) * 2 + c_

    gcol = []
    for i in range(1, 8):
        j = i // 2
        base = (j % 2) * ROWS + grid_row((y + j) % NY, (c + i) % 2) * OWN
        rows = pl.ds(pl.multiple_of(base, OWN), OWN)
        gcol.append(remote(gsum.at[rows], g_col.at[i - 1], gc_ss.at[i - 1], gc_rs.at[i - 1], coldev(i)))

    near_x = (1, NX - 1)
    first, second = slice(0, QTR), slice(QTR, PART)
    ring, direct, summed = [], [], []

    def send_far(h):
        t = term(2, h).astype(BF)
        for n, half in enumerate((first, second)):
            m = 2 * h + n
            far[m] = t[half]
            cp = remote(far.at[m], got_far.at[m], r2_ss.at[m], r2_rs.at[m], xdev(near_x[n]))
            cp.start()
            ring.append(cp)

    def send_near(h):
        for n, (now, later) in enumerate(((second, first), (first, second))):
            m = 2 * h + n
            t = term(near_x[n], h)
            mid[m] = t[later]
            near[m, now] = t[now].astype(BF)
            at = pl.ds(now.start, QTR)
            to = (got_left, got_right)[n]
            cp = remote(near.at[m, at], to.at[h, at], rd_ss.at[m], rd_rs.at[m], xdev(near_x[n]))
            cp.start()
            direct.append(cp)

    def send_sum(h):
        for n, later in enumerate((first, second)):
            m = 2 * h + n
            ring[m].wait_recv()
            near[m, later] = (mid[m] + got_far[m].astype(F32)).astype(BF)
            at = pl.ds(later.start, QTR)
            to = (got_left, got_right)[n]
            cp = remote(near.at[m, at], to.at[h, at], rm_ss.at[m], rm_rs.at[m], xdev(near_x[n]))
            cp.start()
            summed.append(cp)

    send_far(0)
    send_near(0)
    send_far(1)
    share_of = jnp.exp(own_logs - total)
    gsum[...] = (share_of * (sum_g[...] + (own_mean - inner) * sum_w[...])).T.astype(BF)
    for i in COL_ORDER:
        gcol[i - 1].start()
    own[0] = term(0, 0)
    send_sum(0)
    send_near(1)
    own[1] = term(0, 1)
    send_sum(1)

    for cp in gcol:
        cp.wait_recv()
    mine = grid_row(y, c)
    part = gsum[pl.ds(pl.multiple_of(mine * OWN, OWN), OWN), :].astype(F32)
    for i in range(7):
        part = part + g_col[i].astype(F32)
    gz_src[...] = part.astype(BF)
    gzs = [remote(gz_src, g_z.at[i - 1], gz_ss.at[i - 1], gz_rs.at[i - 1], zdev(i)) for i in range(1, NZ)]
    for i in Z_ORDER:
        gzs[i - 1].start()

    out, over, keep, sides_out = [], [], [], {}

    def along(h, b, src, dst):
        for o in (2, 1, 3) if h and b else (1, NX - 1):
            n = 8 * h + NX * b + o
            cp = remote(src, dst, a_ss.at[n], a_rs.at[n], agdev(0, o))
            cp.start()
            if h and b:
                out.append(cp)
            else:
                sides_out[h, b, o] = cp

    def pass_on(h, b):
        for n, o in enumerate(near_x):
            sides_out[h, b, o].wait_recv()
            first_row = (d + b) % 2 * HALF + (s + NX - o) % NX * BLK + h * PART + n * QTR
            half = cg.at[pl.ds(pl.multiple_of(first_row, QTR), QTR)]
            m = 16 + 4 * h + 2 * b + n
            out.append(remote(half, half, a_ss.at[m], a_rs.at[m], agdev(0, o)))
            out[-1].start()


    def spread(h):
        for n in range(2):
            direct[2 * h + n].wait_recv()
            summed[2 * h + n].wait_recv()
        block = own[h] + got_left[h].astype(F32) + got_right[h].astype(F32)
        left, rest = block[:, :HD].astype(BF), block[:, HD:].astype(BF)
        fin[h, 0] = jnp.where(d == 0, left, rest)
        fin[h, 1] = jnp.where(d == 0, rest, left)
        place = cg.at[pl.ds(pl.multiple_of(d * HALF + s * BLK + h * PART, PART), PART)]
        n = 8 * h + NX
        over.append(remote(fin.at[h, 1], place, a_ss.at[n], a_rs.at[n], agdev(1, 0)))
        over[-1].start()
        along(h, 0, fin.at[h, 0], place)
        keep.append(pltpu.make_async_copy(fin.at[h, 0], place, l_sem.at[2 + h]))
        keep[-1].start()

    def relay(h):
        over[h].wait_recv()
        place = cg.at[pl.ds(pl.multiple_of((1 - d) * HALF + s * BLK + h * PART, PART), PART)]
        along(h, 1, place, place)

    spread(0)
    spread(1)
    relay(0)
    pass_on(0, 0)

    for cp in gzs:
        cp.wait_recv()
    for i in range(NZ - 1):
        part = part + g_z[i].astype(F32)
    lg_src[...] = part.astype(BF)
    lg[1 + mine] = lg_src[...]
    back = [
        remote(lg_src, lg.at[1 + mine], lg_ss.at[n], lg_rs.at[n], coldev(i))
        for n, i in enumerate((1, 4, 5))
    ]
    edges = []
    for n, (e, to) in enumerate(((1, 0), (NX - 1, BAND + 1))):
        edges.append([
            remote(lg_src, lg.at[to], e_ss.at[n * 4 + i], e_rs.at[n], edgedev(e, i)) for i in range(4)
        ])
    edge_row = (BAND - 1, 0)
    for n in range(2):

        @pl.when(mine == edge_row[n])
        def _():
            for cp in edges[n]:
                cp.start()

    for cp in back:
        cp.start()
    pass_on(1, 0)
    relay(1)
    pass_on(0, 1)
    for cp in back + [edges[0][0], edges[1][0]]:
        cp.wait_recv()

    @pl.when(s == 0)
    def _():
        lg[0] = jnp.zeros((OWN, D), BF)

    @pl.when(s == NX - 1)
    def _():
        lg[BAND + 1] = jnp.zeros((OWN, D), BF)

    def back_taps(b):
        acc = None
        for a in range(3):
            la = lg[2 - a:2 - a + BAND].reshape(ROWS, D)
            t = nt(la, cw[a, b])
            acc = t if acc is None else acc + t
        return acc

    grad = back_taps(1) + shifted(back_taps(0), -1) + shifted(back_taps(2), 1)
    for h in range(BAND):
        fg[:, h] = grad[h * OWN:(h + 1) * OWN].astype(BF).reshape(IMG, LW, CIN)
    for n in range(2):

        @pl.when(mine == edge_row[n])
        def _():
            for cp in edges[n]:
                cp.wait_send()

    for cp in halo + give_u + give_t + col + zs + ring + direct + summed + gcol + gzs + back + over + list(sides_out.values()):
        cp.wait_send()
    for cp in keep + out:
        cp.wait()


def finish_kernel(factor, cg, fg, out_cg, out_fg, wide, sem):
    parts = wide.shape[0]
    rows = CODES // parts
    gives = [pltpu.make_async_copy(fg, out_fg, sem.at[parts])]
    gives[0].start()
    for n in range(parts):
        at = pl.ds(n * rows, rows)
        wide[n] = cg[at, :].astype(F32) * factor
        gives.append(pltpu.make_async_copy(wide.at[n], out_cg.at[at], sem.at[n]))
        gives[-1].start()
    for cp in gives:
        cp.wait()


def finish(cg, fg, factor):
    parts = 8
    hbm = pl.BlockSpec(memory_space=pl.ANY)
    return pl.pallas_call(
        functools.partial(finish_kernel, factor),
        out_shape=(
            jax.ShapeDtypeStruct(cg.shape, F32),
            jax.ShapeDtypeStruct(fg.shape, BF),
        ),
        in_specs=[pl.BlockSpec(memory_space=pltpu.VMEM)] * 2,
        out_specs=(hbm, hbm),
        scratch_shapes=[
            pltpu.VMEM((parts, CODES // parts, HD), F32),
            pltpu.SemaphoreType.DMA((parts + 1,)),
        ],
        compiler_params=pltpu.CompilerParams(vmem_limit_bytes=40 << 20),
        name="widen",
    )(cg, fg)


def on_device(features, conv_weight, codebook, recon_grad):
    dma = pltpu.SemaphoreType.DMA
    vm = pltpu.VMEM
    hbm = pl.BlockSpec(memory_space=pl.ANY)
    sems = [12, 2, 2, 2, 2, 8, 8, 7, 7, 7, 7, 4, 4, 4, 4, 4, 4, 24, 24, 7, 7, 7, 7, 3, 3, 8, 2]
    cg, fg = pl.pallas_call(
        kernel,
        out_shape=(
            pltpu.VMEM((CODES, HD), BF),
            pltpu.VMEM((IMG, BAND, LW, CIN), BF),
        ),
        in_specs=[hbm] * 4,
        out_specs=(pl.BlockSpec(memory_space=pltpu.VMEM), pl.BlockSpec(memory_space=pltpu.VMEM)),
        scratch_shapes=[
            vm((BAND + 2, IMG, LW, CIN), BF),
            vm((3, 3, CIN, D), BF),
            vm((HALF, D), F32),
            vm((HALF, D), BF),
            vm((HALF, D), BF),
            vm((4 * ROWS // LW, LW, D), BF),
            vm((2 * ROWS // LW, LW, D), BF),
            vm((HALF, 2 * ROWS), F32),
            vm((HALF, 2 * ROWS), F32),
            vm((NX, 1, 2 * ROWS), F32),
            vm((PART, 4 * ROWS), BF),
            vm((HALF, 2 * ROWS), BF),
            vm((HALF, 2 * ROWS), BF),
            vm((D, 2 * ROWS), F32),
            vm((D, 2 * ROWS), F32),
            vm((8, 128), F32),
            vm((7, 8, 128), F32),
            vm((NZ, 8, 128), F32),
            vm((4, QTR, D), BF),
            vm((4, PART, D), BF),
            vm((4, QTR, D), F32),
            vm((4, QTR, D), BF),
            vm((2, PART, D), BF),
            vm((2, PART, D), BF),
            vm((2, PART, D), F32),
            vm((2, 2, PART, HD), BF),
            vm((D, HALF), BF),
            vm((2 * ROWS, D), BF),
            vm((7, OWN, D), BF),
            vm((OWN, D), BF),
            vm((NZ - 1, OWN, D), BF),
            vm((OWN, D), BF),
            vm((BAND + 2, OWN, D), BF),
        ] + [dma((n,)) for n in sems] + [pltpu.SemaphoreType.REGULAR((2,))],
        compiler_params=pltpu.CompilerParams(
            collective_id=0, has_side_effects=True, vmem_limit_bytes=58 << 20
        ),
        cost_estimate=pl.CostEstimate(
            flops=12 * 2**30, bytes_accessed=10 << 20, transcendentals=1 << 21
        ),
        name="soft_quantize",
    )(features, conv_weight, codebook, recon_grad)
    entries_all = codebook.shape[0] * lax.axis_size("code")
    rows_all = ROWS * lax.axis_size("dp") * lax.axis_size("spatial")
    return finish(cg, fg, entries_all / rows_all)


def solution(mesh):
    placed = (P("dp", "spatial", None, None), P(), P("code", None), P("dp", "spatial", None, None))
    return jax.shard_map(
        on_device,
        mesh=mesh,
        in_specs=placed,
        out_specs=(P("code", "dp"), P("dp", "spatial", None, None)),
        check_vma=False,
    )
```

```python
import functools

import jax
import jax.numpy as jnp
from jax import lax
from jax.experimental import pallas as pl
from jax.experimental.pallas import tpu as pltpu
from jax.sharding import PartitionSpec as P

MESH = pl.DeviceIdType.MESH
BF = jnp.bfloat16
F32 = jnp.float32
NX, NY, NZ = 4, 4, 8
IMG, BAND, LW, CIN, D = 4, 4, 16, 512, 256
ROWS = IMG * BAND * LW
CODES = 4096
HALF = CODES // 2
BLK = HALF // NX
PART = BLK // 2
QTR = PART // 2
OWN = IMG * LW
UNIT = OWN // LW
HD = D // 2
COL_ORDER = (5, 4, 3, 7, 2, 6, 1)
Z_ORDER = (4, 3, 5, 2, 6, 1, 7)


def nt(a, b):
    return lax.dot_general(a, b, (((1,), (1,)), ((), ())), preferred_element_type=F32)


def nn(a, b):
    return lax.dot_general(a, b, (((1,), (0,)), ((), ())), preferred_element_type=F32)


def tn(a, b):
    return lax.dot_general(a, b, (((0,), (0,)), ((), ())), preferred_element_type=F32)


def shifted(acc, step):
    rows = acc.shape[0]
    col = lax.broadcasted_iota(jnp.int32, acc.shape, 0) % LW
    keep = (col >= 1) if step == 1 else (col < LW - 1)
    return jnp.where(keep, pltpu.roll(acc, step % rows, 0), 0.0)


def kernel(
    feat, cw_hbm, cb_hbm, up,
    cg, fg,
    xp, cw, cb, hi, lo, right, lat_lo, wts, proj, mst, pg, wb, gb, sum_w, sum_g,
    st, st_col, st_z, far, near, mid, got_far, got_left, got_right, own, fin,
    hi_t, gsum, g_col, gz_src, g_z, lg_src, lg,
    l_sem, h_ss, h_rs, u_ss, u_rs, t_ss, t_rs, sc_ss, sc_rs, sz_ss, sz_rs,
    r2_ss, r2_rs, rd_ss, rd_rs, rm_ss, rm_rs, a_ss, a_rs, gc_ss, gc_rs, gz_ss, gz_rs, lg_ss, lg_rs, e_ss, e_rs, z_sem,
):
    d, s, k = lax.axis_index("dp"), lax.axis_index("spatial"), lax.axis_index("code")
    z, yh, c = k // 4, (k // 2) % 2, k % 2
    y = yh * 2 + d

    def dev(x_, y_, z_, c_):
        return (y_ % 2, x_, z_ * 4 + (y_ // 2) * 2 + c_)

    def xdev(o):
        return dev((s + o) % NX, y, z, c)

    def ydev(j):
        return dev(s, (y + j) % NY, z, c)

    def coldev(i):
        return dev(s, (y + i // 2) % NY, z, (c + i) % 2)

    def zdev(i):
        return dev(s, y, (z + i) % NZ, c)

    def agdev(f, o):
        return ((d + f) % 2, (s + o) % NX, k)

    def edgedev(e, i):
        return dev((s + e) % NX, (y + 2 * (i // 2)) % NY, z, (c + i) % 2)

    def remote(src, dst, ss, rs, who):
        return pltpu.make_async_remote_copy(
            src_ref=src, dst_ref=dst, send_sem=ss, recv_sem=rs,
            device_id=who, device_id_type=MESH,
        )

    load_cb = pltpu.make_async_copy(cb_hbm.at[pl.ds(d * HALF, HALF)], cb, l_sem.at[0])
    load_u = [
        pltpu.make_async_copy(up.at[:, h], right.at[pl.ds(h * UNIT, UNIT)], l_sem.at[4 + h])
        for h in range(BAND)
    ]
    load_x = [
        pltpu.make_async_copy(feat.at[:, h], xp.at[1 + h], l_sem.at[8 + h]) for h in range(BAND)
    ]
    load_w = pltpu.make_async_copy(cw_hbm, cw, l_sem.at[1])
    barrier = pltpu.get_barrier_semaphore()
    peers = [xdev(1), xdev(NX - 1), ydev(1), ydev(NY - 1), zdev(1), zdev(NZ - 1)]
    peers.append(dev(s, y, z, 1 - c))
    for who in peers:
        pl.semaphore_signal(barrier, inc=1, device_id=who, device_id_type=MESH)
    for cp in load_u + load_x + [load_w, load_cb]:
        cp.start()
    pl.semaphore_wait(barrier, len(peers))

    halo = [
        remote(feat.at[:, BAND - 1], xp.at[0], h_ss.at[0], h_rs.at[0], xdev(1)),
        remote(feat.at[:, 0], xp.at[BAND + 1], h_ss.at[1], h_rs.at[1], xdev(NX - 1)),
    ]
    sides = (1, NY - 1)

    def share(buf, at, count, peer_at, ss, rs, n):
        return remote(
            buf.at[pl.ds(at, count)], buf.at[pl.ds(peer_at, count)], ss.at[n], rs.at[n], ydev(sides[n % 2])
        )

    quarter = ROWS // LW
    give_u = [
        share(right, n * 2 * UNIT, 2 * UNIT, quarter + n * 2 * UNIT, u_ss, u_rs, n) for n in range(2)
    ]
    for cp in halo:
        cp.start()
    for cp in load_u:
        cp.wait()
    for cp in give_u:
        cp.start()

    def tell(n, reach):
        for i in (reach, NZ - reach):
            pl.semaphore_signal(z_sem.at[n], inc=1, device_id=zdev(i), device_id_type=MESH)

    tell(0, 1)

    def rows_of(buf, n):
        return buf[n * quarter:(n + 1) * quarter].reshape(ROWS, D)

    def project(rb):
        u = rows_of(right, rb)
        for i in range(NX):
            rows = slice(i * BLK, (i + 1) * BLK)
            proj[rows, rb * ROWS:(rb + 1) * ROWS] = nt(hi[rows, :], u) + nt(lo[rows, :], u)

    give_t = []

    def convolve(grid_rows):
        def taps(b):
            acc = None
            for a in range(3):
                xa = jnp.concatenate([xp[h + a].reshape(OWN, CIN) for h in grid_rows], axis=0)
                t = nn(xa, cw[a, b])
                acc = t if acc is None else acc + t
            return acc

        latent = taps(1) + shifted(taps(0), 1) + shifted(taps(2), -1)
        lat_hi = latent.astype(BF)
        rest = (latent - lat_hi.astype(F32)).astype(BF)
        for n, h in enumerate(grid_rows):
            at = slice(n * OWN, (n + 1) * OWN)
            right[2 * quarter + h * UNIT:2 * quarter + (h + 1) * UNIT] = lat_hi[at].reshape(UNIT, LW, D)
            lat_lo[h * UNIT:(h + 1) * UNIT] = rest[at].reshape(UNIT, LW, D)
        for n, h in enumerate(grid_rows):
            m = len(give_t)
            give_t.append(share(right, 2 * quarter + h * UNIT, UNIT, 3 * quarter + h * UNIT, t_ss, t_rs, m))
            give_t[-1].start()
        for n, h in enumerate(grid_rows):
            m = len(give_t)
            give_t.append(share(lat_lo, h * UNIT, UNIT, quarter + h * UNIT, t_ss, t_rs, m))
            give_t[-1].start()

    for cp in load_x + [load_w]:
        cp.wait()
    convolve((1, 2))
    load_cb.wait()

    @pl.loop(0, HALF // 256)
    def _(i):
        rows = pl.ds(pl.multiple_of(i * 256, 256), 256)
        v = cb[rows, :]
        h = v.astype(BF)
        hi[rows, :] = h
        lo[rows, :] = (v - h.astype(F32)).astype(BF)

    project(0)

    pl.semaphore_wait(z_sem.at[0], 2)
    tell(1, 2)
    for cp in halo + give_u:
        cp.wait_recv()

    @pl.when(s == 0)
    def _():
        xp[0] = jnp.zeros((IMG, LW, CIN), BF)

    @pl.when(s == NX - 1)
    def _():
        xp[BAND + 1] = jnp.zeros((IMG, LW, CIN), BF)

    convolve((0, BAND - 1))

    def merge(a, b):
        top = jnp.maximum(a[0], b[0])
        ea, eb = jnp.exp(a[0] - top), jnp.exp(b[0] - top)
        return top, a[1] * ea + b[1] * eb, a[2] * ea + b[2] * eb

    def score(rb):
        cols = slice(rb * ROWS, (rb + 1) * ROWS)
        lh = rows_of(right, 2 + rb)
        ll = rows_of(lat_lo, rb)

        def step(i, carry):
            rows = slice(i * BLK, (i + 1) * BLK)
            h = hi[rows, :]
            sc = nt(h, lh) + (nt(h, ll) + nt(lo[rows, :], lh))
            top = jnp.max(sc, axis=0, keepdims=True)
            w = jnp.exp(sc - top)
            wts[rows, cols] = w
            mst[i, :, cols] = top
            mass = jnp.sum(w, axis=0, keepdims=True)
            dots = jnp.sum(w * proj[rows, cols], axis=0, keepdims=True)
            return merge(carry, (top, mass, dots))

        zero = jnp.zeros((1, ROWS), F32)
        carry = (zero - 3.0e38, zero, zero)
        for i in range(NX):
            carry = step(i, carry)
        top, mass, dots = carry
        logs, mean = top + jnp.log(mass), dots / mass
        for n in range(2):
            st[2 * rb + n:2 * rb + n + 1, :] = logs[:, n * 128:(n + 1) * 128]
            st[4 + 2 * rb + n:5 + 2 * rb + n, :] = mean[:, n * 128:(n + 1) * 128]
        return logs, mean

    ends = [score(0)]
    pl.semaphore_wait(z_sem.at[1], 2)
    project(1)
    for cp in give_t:
        cp.wait_recv()
    ends.append(score(1))

    def combine(parts):
        top = functools.reduce(jnp.maximum, [p[:4] for p in parts])
        mass, dots = 0.0, 0.0
        for p in parts:
            e = jnp.exp(p[:4] - top)
            mass, dots = mass + e, dots + e * p[4:]
        return top + jnp.log(mass), dots / mass

    def swap(p):
        return jnp.concatenate([p[2:4], p[0:2], p[6:8], p[4:6]], axis=0)

    col = [remote(st, st_col.at[i - 1], sc_ss.at[i - 1], sc_rs.at[i - 1], coldev(i)) for i in range(1, 8)]
    for i in COL_ORDER:
        col[i - 1].start()

    @pl.loop(0, HALF // 256)
    def _(i):
        at = pl.ds(pl.multiple_of(i * 256, 256), 256)
        hi_t[:, at] = hi[at, :].T

    own_logs = jnp.concatenate([e[0] for e in ends], axis=1)
    own_mean = jnp.concatenate([e[1] for e in ends], axis=1)
    for i in range(2 * NX):
        rows = slice(i * PART, (i + 1) * PART)
        w = wts[rows, :] * jnp.exp(mst[i // 2] - own_logs)
        wb[rows, :] = w.astype(BF)
        gb[rows, :] = (w * (proj[rows, :] - own_mean)).astype(BF)

    for cp in col:
        cp.wait_recv()
    parts = [st[...]]
    for i in range(1, 8):
        p = st_col[i - 1]
        parts.append(swap(p) if (i // 2) % 2 else p)
    logs, mean = combine(parts)
    st_z[0] = jnp.concatenate([logs, mean], axis=0)
    zs = [remote(st_z.at[0], st_z.at[i], sz_ss.at[i - 1], sz_rs.at[i - 1], zdev(i)) for i in range(1, NZ)]
    for i in Z_ORDER:
        zs[i - 1].start()
    sum_g[...] = nn(hi_t[...], gb[...])
    sum_w[...] = nn(hi_t[...], wb[...])
    for cp in zs:
        cp.wait_recv()
    logs, mean = combine([st_z[i] for i in range(NZ)])
    total = jnp.concatenate([logs[n:n + 1] for n in range(4)], axis=1)
    inner = jnp.concatenate([mean[n:n + 1] for n in range(4)], axis=1)

    both = 2 * ROWS

    def term(o, h):
        blk = (s + o) % NX
        rows = pl.ds(pl.multiple_of(blk * BLK + h * PART, PART), PART)
        p = wts[rows, :] * jnp.exp(mst[blk] - total)
        g = (p * (proj[rows, :] - inner)).astype(BF)
        pg[:, :both] = p.astype(BF)
        pg[:, both:] = g
        return nn(pg[...], right[...].reshape(4 * ROWS, D))

    def grid_row(y_, c_):
        return (y_ // 2) * 2 + c_

    gcol = []
    for i in range(1, 8):
        j = i // 2
        base = (j % 2) * ROWS + grid_row((y + j) % NY, (c + i) % 2) * OWN
        rows = pl.ds(pl.multiple_of(base, OWN), OWN)
        gcol.append(remote(gsum.at[rows], g_col.at[i - 1], gc_ss.at[i - 1], gc_rs.at[i - 1], coldev(i)))

    near_x = (1, NX - 1)
    first, second = slice(0, QTR), slice(QTR, PART)
    ring, direct, summed = [], [], []

    def send_far(h):
        t = term(2, h).astype(BF)
        for n, half in enumerate((first, second)):
            m = 2 * h + n
            far[m] = t[half]
            cp = remote(far.at[m], got_far.at[m], r2_ss.at[m], r2_rs.at[m], xdev(near_x[n]))
            cp.start()
            ring.append(cp)

    def send_near(h):
        for n, (now, later) in enumerate(((second, first), (first, second))):
            m = 2 * h + n
            t = term(near_x[n], h)
            mid[m] = t[later]
            near[m, now] = t[now].astype(BF)
            at = pl.ds(now.start, QTR)
            to = (got_left, got_right)[n]
            cp = remote(near.at[m, at], to.at[h, at], rd_ss.at[m], rd_rs.at[m], xdev(near_x[n]))
            cp.start()
            direct.append(cp)

    def send_sum(h):
        for n, later in enumerate((first, second)):
            m = 2 * h + n
            ring[m].wait_recv()
            near[m, later] = (mid[m] + got_far[m].astype(F32)).astype(BF)
            at = pl.ds(later.start, QTR)
            to = (got_left, got_right)[n]
            cp = remote(near.at[m, at], to.at[h, at], rm_ss.at[m], rm_rs.at[m], xdev(near_x[n]))
            cp.start()
            summed.append(cp)

    send_far(0)
    share_of = jnp.exp(own_logs - total)
    gsum[...] = (share_of * (sum_g[...] + (own_mean - inner) * sum_w[...])).T.astype(BF)
    for i in COL_ORDER:
        gcol[i - 1].start()
    send_near(0)
    send_far(1)
    own[0] = term(0, 0)
    send_sum(0)
    send_near(1)
    own[1] = term(0, 1)
    send_sum(1)

    for cp in gcol:
        cp.wait_recv()
    mine = grid_row(y, c)
    part = gsum[pl.ds(pl.multiple_of(mine * OWN, OWN), OWN), :].astype(F32)
    for i in range(7):
        part = part + g_col[i].astype(F32)
    gz_src[...] = part.astype(BF)
    gzs = [remote(gz_src, g_z.at[i - 1], gz_ss.at[i - 1], gz_rs.at[i - 1], zdev(i)) for i in range(1, NZ)]
    for i in Z_ORDER:
        gzs[i - 1].start()

    out, over, keep, sides_out = [], [], [], {}

    def along(h, b, src, dst):
        for o in (2, 1, 3) if h and b else (1, NX - 1):
            n = 8 * h + NX * b + o
            cp = remote(src, dst, a_ss.at[n], a_rs.at[n], agdev(0, o))
            cp.start()
            if h and b:
                out.append(cp)
            else:
                sides_out[h, b, o] = cp

    def pass_on(h, b):
        for n, o in enumerate(near_x):
            sides_out[h, b, o].wait_recv()
            first_row = (d + b) % 2 * HALF + (s + NX - o) % NX * BLK + h * PART + n * QTR
            half = cg.at[pl.ds(pl.multiple_of(first_row, QTR), QTR)]
            m = 16 + 4 * h + 2 * b + n
            out.append(remote(half, half, a_ss.at[m], a_rs.at[m], agdev(0, o)))
            out[-1].start()


    def spread(h):
        for n in range(2):
            direct[2 * h + n].wait_recv()
            summed[2 * h + n].wait_recv()
        block = own[h] + got_left[h].astype(F32) + got_right[h].astype(F32)
        left, rest = block[:, :HD].astype(BF), block[:, HD:].astype(BF)
        fin[h, 0] = jnp.where(d == 0, left, rest)
        fin[h, 1] = jnp.where(d == 0, rest, left)
        place = cg.at[pl.ds(pl.multiple_of(d * HALF + s * BLK + h * PART, PART), PART)]
        n = 8 * h + NX
        over.append(remote(fin.at[h, 1], place, a_ss.at[n], a_rs.at[n], agdev(1, 0)))
        over[-1].start()
        along(h, 0, fin.at[h, 0], place)
        keep.append(pltpu.make_async_copy(fin.at[h, 0], place, l_sem.at[2 + h]))
        keep[-1].start()

    def relay(h):
        over[h].wait_recv()
        place = cg.at[pl.ds(pl.multiple_of((1 - d) * HALF + s * BLK + h * PART, PART), PART)]
        along(h, 1, place, place)

    spread(0)
    spread(1)
    relay(0)
    pass_on(0, 0)

    for cp in gzs:
        cp.wait_recv()
    for i in range(NZ - 1):
        part = part + g_z[i].astype(F32)
    lg_src[...] = part.astype(BF)
    lg[1 + mine] = lg_src[...]
    back = [
        remote(lg_src, lg.at[1 + mine], lg_ss.at[n], lg_rs.at[n], coldev(i))
        for n, i in enumerate((1, 4, 5))
    ]
    edges = []
    for n, (e, to) in enumerate(((1, 0), (NX - 1, BAND + 1))):
        edges.append([
            remote(lg_src, lg.at[to], e_ss.at[n * 4 + i], e_rs.at[n], edgedev(e, i)) for i in range(4)
        ])
    edge_row = (BAND - 1, 0)
    for n in range(2):

        @pl.when(mine == edge_row[n])
        def _():
            for cp in edges[n]:
                cp.start()

    for cp in back:
        cp.start()
    pass_on(1, 0)
    relay(1)
    pass_on(0, 1)
    for cp in back + [edges[0][0], edges[1][0]]:
        cp.wait_recv()

    @pl.when(s == 0)
    def _():
        lg[0] = jnp.zeros((OWN, D), BF)

    @pl.when(s == NX - 1)
    def _():
        lg[BAND + 1] = jnp.zeros((OWN, D), BF)

    def back_taps(b):
        acc = None
        for a in range(3):
            la = lg[2 - a:2 - a + BAND].reshape(ROWS, D)
            t = nt(la, cw[a, b])
            acc = t if acc is None else acc + t
        return acc

    grad = back_taps(1) + shifted(back_taps(0), -1) + shifted(back_taps(2), 1)
    for h in range(BAND):
        fg[:, h] = grad[h * OWN:(h + 1) * OWN].astype(BF).reshape(IMG, LW, CIN)
    for n in range(2):

        @pl.when(mine == edge_row[n])
        def _():
            for cp in edges[n]:
                cp.wait_send()

    for cp in halo + give_u + give_t + col + zs + ring + direct + summed + gcol + gzs + back + over + list(sides_out.values()):
        cp.wait_send()
    for cp in keep + out:
        cp.wait()


def finish_kernel(factor, cg, fg, out_cg, out_fg, wide, sem):
    parts = wide.shape[0]
    rows = CODES // parts
    gives = [pltpu.make_async_copy(fg, out_fg, sem.at[parts])]
    gives[0].start()
    for n in range(parts):
        at = pl.ds(n * rows, rows)
        wide[n] = cg[at, :].astype(F32) * factor
        gives.append(pltpu.make_async_copy(wide.at[n], out_cg.at[at], sem.at[n]))
        gives[-1].start()
    for cp in gives:
        cp.wait()


def finish(cg, fg, factor):
    parts = 8
    hbm = pl.BlockSpec(memory_space=pl.ANY)
    return pl.pallas_call(
        functools.partial(finish_kernel, factor),
        out_shape=(
            jax.ShapeDtypeStruct(cg.shape, F32),
            jax.ShapeDtypeStruct(fg.shape, BF),
        ),
        in_specs=[pl.BlockSpec(memory_space=pltpu.VMEM)] * 2,
        out_specs=(hbm, hbm),
        scratch_shapes=[
            pltpu.VMEM((parts, CODES // parts, HD), F32),
            pltpu.SemaphoreType.DMA((parts + 1,)),
        ],
        compiler_params=pltpu.CompilerParams(vmem_limit_bytes=40 << 20),
        name="widen",
    )(cg, fg)


def on_device(features, conv_weight, codebook, recon_grad):
    dma = pltpu.SemaphoreType.DMA
    vm = pltpu.VMEM
    hbm = pl.BlockSpec(memory_space=pl.ANY)
    sems = [12, 2, 2, 2, 2, 8, 8, 7, 7, 7, 7, 4, 4, 4, 4, 4, 4, 24, 24, 7, 7, 7, 7, 3, 3, 8, 2]
    cg, fg = pl.pallas_call(
        kernel,
        out_shape=(
            pltpu.VMEM((CODES, HD), BF),
            pltpu.VMEM((IMG, BAND, LW, CIN), BF),
        ),
        in_specs=[hbm] * 4,
        out_specs=(pl.BlockSpec(memory_space=pltpu.VMEM), pl.BlockSpec(memory_space=pltpu.VMEM)),
        scratch_shapes=[
            vm((BAND + 2, IMG, LW, CIN), BF),
            vm((3, 3, CIN, D), BF),
            vm((HALF, D), F32),
            vm((HALF, D), BF),
            vm((HALF, D), BF),
            vm((4 * ROWS // LW, LW, D), BF),
            vm((2 * ROWS // LW, LW, D), BF),
            vm((HALF, 2 * ROWS), F32),
            vm((HALF, 2 * ROWS), F32),
            vm((NX, 1, 2 * ROWS), F32),
            vm((PART, 4 * ROWS), BF),
            vm((HALF, 2 * ROWS), BF),
            vm((HALF, 2 * ROWS), BF),
            vm((D, 2 * ROWS), F32),
            vm((D, 2 * ROWS), F32),
            vm((8, 128), F32),
            vm((7, 8, 128), F32),
            vm((NZ, 8, 128), F32),
            vm((4, QTR, D), BF),
            vm((4, PART, D), BF),
            vm((4, QTR, D), F32),
            vm((4, QTR, D), BF),
            vm((2, PART, D), BF),
            vm((2, PART, D), BF),
            vm((2, PART, D), F32),
            vm((2, 2, PART, HD), BF),
            vm((D, HALF), BF),
            vm((2 * ROWS, D), BF),
            vm((7, OWN, D), BF),
            vm((OWN, D), BF),
            vm((NZ - 1, OWN, D), BF),
            vm((OWN, D), BF),
            vm((BAND + 2, OWN, D), BF),
        ] + [dma((n,)) for n in sems] + [pltpu.SemaphoreType.REGULAR((2,))],
        compiler_params=pltpu.CompilerParams(
            collective_id=0, has_side_effects=True, vmem_limit_bytes=58 << 20
        ),
        cost_estimate=pl.CostEstimate(
            flops=12 * 2**30, bytes_accessed=10 << 20, transcendentals=1 << 21
        ),
        name="soft_quantize",
    )(features, conv_weight, codebook, recon_grad)
    entries_all = codebook.shape[0] * lax.axis_size("code")
    rows_all = ROWS * lax.axis_size("dp") * lax.axis_size("spatial")
    return finish(cg, fg, entries_all / rows_all)


def solution(mesh):
    placed = (P("dp", "spatial", None, None), P(), P("code", None), P("dp", "spatial", None, None))
    return jax.shard_map(
        on_device,
        mesh=mesh,
        in_specs=placed,
        out_specs=(P("code", "dp"), P("dp", "spatial", None, None)),
        check_vma=False,
    )
```

```python
import functools

import jax
import jax.numpy as jnp
from jax import lax
from jax.experimental import pallas as pl
from jax.experimental.pallas import tpu as pltpu
from jax.sharding import PartitionSpec as P

MESH = pl.DeviceIdType.MESH
BF = jnp.bfloat16
F32 = jnp.float32
NX, NY, NZ = 4, 4, 8
IMG, BAND, LW, CIN, D = 4, 4, 16, 512, 256
ROWS = IMG * BAND * LW
CODES = 4096
HALF = CODES // 2
BLK = HALF // NX
PART = BLK // 2
QTR = PART // 2
OWN = IMG * LW
UNIT = OWN // LW
HD = D // 2
COL_ORDER = (5, 4, 3, 7, 2, 6, 1)
Z_ORDER = (4, 3, 5, 2, 6, 1, 7)


def nt(a, b):
    return lax.dot_general(a, b, (((1,), (1,)), ((), ())), preferred_element_type=F32)


def nn(a, b):
    return lax.dot_general(a, b, (((1,), (0,)), ((), ())), preferred_element_type=F32)


def tn(a, b):
    return lax.dot_general(a, b, (((0,), (0,)), ((), ())), preferred_element_type=F32)


def shifted(acc, step):
    rows = acc.shape[0]
    col = lax.broadcasted_iota(jnp.int32, acc.shape, 0) % LW
    keep = (col >= 1) if step == 1 else (col < LW - 1)
    return jnp.where(keep, pltpu.roll(acc, step % rows, 0), 0.0)


def kernel(
    feat, cw_hbm, cb_hbm, up,
    cg, fg,
    xp, cw, cb, hi, lo, right, lat_lo, wts, proj, mst, pg, wb, gb, sum_w, sum_g,
    st, st_col, st_z, far, near, mid, got_far, got_left, got_right, own, fin,
    hi_t, gsum, g_col, gz_src, g_z, lg_src, lg,
    l_sem, h_ss, h_rs, u_ss, u_rs, t_ss, t_rs, sc_ss, sc_rs, sz_ss, sz_rs,
    r2_ss, r2_rs, rd_ss, rd_rs, rm_ss, rm_rs, a_ss, a_rs, gc_ss, gc_rs, gz_ss, gz_rs, lg_ss, lg_rs, e_ss, e_rs, z_sem,
):
    d, s, k = lax.axis_index("dp"), lax.axis_index("spatial"), lax.axis_index("code")
    z, yh, c = k // 4, (k // 2) % 2, k % 2
    y = yh * 2 + d

    def dev(x_, y_, z_, c_):
        return (y_ % 2, x_, z_ * 4 + (y_ // 2) * 2 + c_)

    def xdev(o):
        return dev((s + o) % NX, y, z, c)

    def ydev(j):
        return dev(s, (y + j) % NY, z, c)

    def coldev(i):
        return dev(s, (y + i // 2) % NY, z, (c + i) % 2)

    def zdev(i):
        return dev(s, y, (z + i) % NZ, c)

    def agdev(f, o):
        return ((d + f) % 2, (s + o) % NX, k)

    def edgedev(e, i):
        return dev((s + e) % NX, (y + 2 * (i // 2)) % NY, z, (c + i) % 2)

    def remote(src, dst, ss, rs, who):
        return pltpu.make_async_remote_copy(
            src_ref=src, dst_ref=dst, send_sem=ss, recv_sem=rs,
            device_id=who, device_id_type=MESH,
        )

    load_cb = pltpu.make_async_copy(cb_hbm.at[pl.ds(d * HALF, HALF)], cb, l_sem.at[0])
    load_u = [
        pltpu.make_async_copy(up.at[:, h], right.at[pl.ds(h * UNIT, UNIT)], l_sem.at[4 + h])
        for h in range(BAND)
    ]
    load_x = [
        pltpu.make_async_copy(feat.at[:, h], xp.at[1 + h], l_sem.at[8 + h]) for h in range(BAND)
    ]
    load_w = pltpu.make_async_copy(cw_hbm, cw, l_sem.at[1])
    barrier = pltpu.get_barrier_semaphore()
    peers = [xdev(1), xdev(NX - 1), ydev(1), ydev(NY - 1), zdev(1), zdev(NZ - 1)]
    peers.append(dev(s, y, z, 1 - c))
    for who in peers:
        pl.semaphore_signal(barrier, inc=1, device_id=who, device_id_type=MESH)
    for cp in load_u + load_x + [load_w, load_cb]:
        cp.start()
    pl.semaphore_wait(barrier, len(peers))

    halo = [
        remote(feat.at[:, BAND - 1], xp.at[0], h_ss.at[0], h_rs.at[0], xdev(1)),
        remote(feat.at[:, 0], xp.at[BAND + 1], h_ss.at[1], h_rs.at[1], xdev(NX - 1)),
    ]
    sides = (1, NY - 1)

    def share(buf, at, count, peer_at, ss, rs, n):
        return remote(
            buf.at[pl.ds(at, count)], buf.at[pl.ds(peer_at, count)], ss.at[n], rs.at[n], ydev(sides[n % 2])
        )

    quarter = ROWS // LW
    give_u = [
        share(right, n * 2 * UNIT, 2 * UNIT, quarter + n * 2 * UNIT, u_ss, u_rs, n) for n in range(2)
    ]
    for cp in halo:
        cp.start()
    for cp in load_u:
        cp.wait()
    for cp in give_u:
        cp.start()

    def tell(n, reach):
        for i in (reach, NZ - reach):
            pl.semaphore_signal(z_sem.at[n], inc=1, device_id=zdev(i), device_id_type=MESH)

    tell(0, 1)

    def rows_of(buf, n):
        return buf[n * quarter:(n + 1) * quarter].reshape(ROWS, D)

    def project(rb):
        u = rows_of(right, rb)
        for i in range(NX):
            rows = slice(i * BLK, (i + 1) * BLK)
            proj[rows, rb * ROWS:(rb + 1) * ROWS] = nt(hi[rows, :], u) + nt(lo[rows, :], u)

    give_t = []

    def convolve(grid_rows):
        def taps(b):
            acc = None
            for a in range(3):
                xa = jnp.concatenate([xp[h + a].reshape(OWN, CIN) for h in grid_rows], axis=0)
                t = nn(xa, cw[a, b])
                acc = t if acc is None else acc + t
            return acc

        latent = taps(1) + shifted(taps(0), 1) + shifted(taps(2), -1)
        lat_hi = latent.astype(BF)
        rest = (latent - lat_hi.astype(F32)).astype(BF)
        for n, h in enumerate(grid_rows):
            at = slice(n * OWN, (n + 1) * OWN)
            right[2 * quarter + h * UNIT:2 * quarter + (h + 1) * UNIT] = lat_hi[at].reshape(UNIT, LW, D)
            lat_lo[h * UNIT:(h + 1) * UNIT] = rest[at].reshape(UNIT, LW, D)
        for n, h in enumerate(grid_rows):
            m = len(give_t)
            give_t.append(share(right, 2 * quarter + h * UNIT, UNIT, 3 * quarter + h * UNIT, t_ss, t_rs, m))
            give_t[-1].start()
        for n, h in enumerate(grid_rows):
            m = len(give_t)
            give_t.append(share(lat_lo, h * UNIT, UNIT, quarter + h * UNIT, t_ss, t_rs, m))
            give_t[-1].start()

    for cp in load_x + [load_w]:
        cp.wait()
    convolve((1, 2))
    load_cb.wait()

    @pl.loop(0, HALF // 256)
    def _(i):
        rows = pl.ds(pl.multiple_of(i * 256, 256), 256)
        v = cb[rows, :]
        h = v.astype(BF)
        hi[rows, :] = h
        lo[rows, :] = (v - h.astype(F32)).astype(BF)

    project(0)

    pl.semaphore_wait(z_sem.at[0], 2)
    tell(1, 2)
    for cp in halo + give_u:
        cp.wait_recv()

    @pl.when(s == 0)
    def _():
        xp[0] = jnp.zeros((IMG, LW, CIN), BF)

    @pl.when(s == NX - 1)
    def _():
        xp[BAND + 1] = jnp.zeros((IMG, LW, CIN), BF)

    convolve((0, BAND - 1))

    def merge(a, b):
        top = jnp.maximum(a[0], b[0])
        ea, eb = jnp.exp(a[0] - top), jnp.exp(b[0] - top)
        return top, a[1] * ea + b[1] * eb, a[2] * ea + b[2] * eb

    def score(rb):
        cols = slice(rb * ROWS, (rb + 1) * ROWS)
        lh = rows_of(right, 2 + rb)
        ll = rows_of(lat_lo, rb)

        def step(i, carry):
            rows = slice(i * BLK, (i + 1) * BLK)
            h = hi[rows, :]
            sc = nt(h, lh) + (nt(h, ll) + nt(lo[rows, :], lh))
            top = jnp.max(sc, axis=0, keepdims=True)
            w = jnp.exp(sc - top)
            wts[rows, cols] = w
            mst[i, :, cols] = top
            mass = jnp.sum(w, axis=0, keepdims=True)
            dots = jnp.sum(w * proj[rows, cols], axis=0, keepdims=True)
            return merge(carry, (top, mass, dots))

        zero = jnp.zeros((1, ROWS), F32)
        carry = (zero - 3.0e38, zero, zero)
        for i in range(NX):
            carry = step(i, carry)
        top, mass, dots = carry
        logs, mean = top + jnp.log(mass), dots / mass
        for n in range(2):
            st[2 * rb + n:2 * rb + n + 1, :] = logs[:, n * 128:(n + 1) * 128]
            st[4 + 2 * rb + n:5 + 2 * rb + n, :] = mean[:, n * 128:(n + 1) * 128]
        return logs, mean

    ends = [score(0)]
    pl.semaphore_wait(z_sem.at[1], 2)
    project(1)
    for cp in give_t:
        cp.wait_recv()
    ends.append(score(1))

    def combine(parts):
        top = functools.reduce(jnp.maximum, [p[:4] for p in parts])
        mass, dots = 0.0, 0.0
        for p in parts:
            e = jnp.exp(p[:4] - top)
            mass, dots = mass + e, dots + e * p[4:]
        return top + jnp.log(mass), dots / mass

    def swap(p):
        return jnp.concatenate([p[2:4], p[0:2], p[6:8], p[4:6]], axis=0)

    col = [remote(st, st_col.at[i - 1], sc_ss.at[i - 1], sc_rs.at[i - 1], coldev(i)) for i in range(1, 8)]
    for i in COL_ORDER:
        col[i - 1].start()

    @pl.loop(0, HALF // 256)
    def _(i):
        at = pl.ds(pl.multiple_of(i * 256, 256), 256)
        hi_t[:, at] = hi[at, :].T

    own_logs = jnp.concatenate([e[0] for e in ends], axis=1)
    own_mean = jnp.concatenate([e[1] for e in ends], axis=1)
    for i in range(2 * NX):
        rows = slice(i * PART, (i + 1) * PART)
        w = wts[rows, :] * jnp.exp(mst[i // 2] - own_logs)
        wb[rows, :] = w.astype(BF)
        gb[rows, :] = (w * (proj[rows, :] - own_mean)).astype(BF)

    for cp in col:
        cp.wait_recv()
    parts = [st[...]]
    for i in range(1, 8):
        p = st_col[i - 1]
        parts.append(swap(p) if (i // 2) % 2 else p)
    logs, mean = combine(parts)
    st_z[0] = jnp.concatenate([logs, mean], axis=0)
    zs = [remote(st_z.at[0], st_z.at[i], sz_ss.at[i - 1], sz_rs.at[i - 1], zdev(i)) for i in range(1, NZ)]
    for i in Z_ORDER:
        zs[i - 1].start()
    sum_g[...] = nn(hi_t[...], gb[...])
    sum_w[...] = nn(hi_t[...], wb[...])
    for cp in zs:
        cp.wait_recv()
    logs, mean = combine([st_z[i] for i in range(NZ)])
    total = jnp.concatenate([logs[n:n + 1] for n in range(4)], axis=1)
    inner = jnp.concatenate([mean[n:n + 1] for n in range(4)], axis=1)

    both = 2 * ROWS

    def term(o, h):
        blk = (s + o) % NX
        rows = pl.ds(pl.multiple_of(blk * BLK + h * PART, PART), PART)
        p = wts[rows, :] * jnp.exp(mst[blk] - total)
        g = (p * (proj[rows, :] - inner)).astype(BF)
        pg[:, :both] = p.astype(BF)
        pg[:, both:] = g
        return nn(pg[...], right[...].reshape(4 * ROWS, D))

    def grid_row(y_, c_):
        return (y_ // 2) * 2 + c_

    gcol = []
    for i in range(1, 8):
        j = i // 2
        base = (j % 2) * ROWS + grid_row((y + j) % NY, (c + i) % 2) * OWN
        rows = pl.ds(pl.multiple_of(base, OWN), OWN)
        gcol.append(remote(gsum.at[rows], g_col.at[i - 1], gc_ss.at[i - 1], gc_rs.at[i - 1], coldev(i)))

    near_x = (1, NX - 1)
    first, second = slice(0, QTR), slice(QTR, PART)
    ring, direct, summed = [], [], []

    def send_far(h):
        t = term(2, h).astype(BF)
        for n, half in enumerate((first, second)):
            m = 2 * h + n
            far[m] = t[half]
            cp = remote(far.at[m], got_far.at[m], r2_ss.at[m], r2_rs.at[m], xdev(near_x[n]))
            cp.start()
            ring.append(cp)

    def send_near(h):
        for n, (now, later) in enumerate(((second, first), (first, second))):
            m = 2 * h + n
            t = term(near_x[n], h)
            mid[m] = t[later]
            near[m, now] = t[now].astype(BF)
            at = pl.ds(now.start, QTR)
            to = (got_left, got_right)[n]
            cp = remote(near.at[m, at], to.at[h, at], rd_ss.at[m], rd_rs.at[m], xdev(near_x[n]))
            cp.start()
            direct.append(cp)

    def send_sum(h):
        for n, later in enumerate((first, second)):
            m = 2 * h + n
            ring[m].wait_recv()
            near[m, later] = (mid[m] + got_far[m].astype(F32)).astype(BF)
            at = pl.ds(later.start, QTR)
            to = (got_left, got_right)[n]
            cp = remote(near.at[m, at], to.at[h, at], rm_ss.at[m], rm_rs.at[m], xdev(near_x[n]))
            cp.start()
            summed.append(cp)

    send_far(0)
    share_of = jnp.exp(own_logs - total)
    gsum[...] = (share_of * (sum_g[...] + (own_mean - inner) * sum_w[...])).T.astype(BF)
    for i in COL_ORDER:
        gcol[i - 1].start()
    send_near(0)
    send_far(1)
    own[0] = term(0, 0)
    send_sum(0)
    send_near(1)
    own[1] = term(0, 1)
    send_sum(1)

    for cp in gcol:
        cp.wait_recv()
    mine = grid_row(y, c)
    part = gsum[pl.ds(pl.multiple_of(mine * OWN, OWN), OWN), :].astype(F32)
    for i in range(7):
        part = part + g_col[i].astype(F32)
    gz_src[...] = part.astype(BF)
    gzs = [remote(gz_src, g_z.at[i - 1], gz_ss.at[i - 1], gz_rs.at[i - 1], zdev(i)) for i in range(1, NZ)]
    for i in Z_ORDER:
        gzs[i - 1].start()

    out, over, keep, sides_out = [], [], [], {}

    def along(h, b, src, dst):
        for o in (2, 1, 3) if h and b else (1, NX - 1):
            n = 8 * h + NX * b + o
            cp = remote(src, dst, a_ss.at[n], a_rs.at[n], agdev(0, o))
            cp.start()
            if h and b:
                out.append(cp)
            else:
                sides_out[h, b, o] = cp

    def pass_on(h, b):
        for n, o in enumerate(near_x):
            sides_out[h, b, o].wait_recv()
            first_row = (d + b) % 2 * HALF + (s + NX - o) % NX * BLK + h * PART + n * QTR
            half = cg.at[pl.ds(pl.multiple_of(first_row, QTR), QTR)]
            m = 16 + 4 * h + 2 * b + n
            out.append(remote(half, half, a_ss.at[m], a_rs.at[m], agdev(0, o)))
            out[-1].start()


    def spread(h):
        for n in range(2):
            direct[2 * h + n].wait_recv()
            summed[2 * h + n].wait_recv()
        block = own[h] + got_left[h].astype(F32) + got_right[h].astype(F32)
        left, rest = block[:, :HD].astype(BF), block[:, HD:].astype(BF)
        fin[h, 0] = jnp.where(d == 0, left, rest)
        fin[h, 1] = jnp.where(d == 0, rest, left)
        place = cg.at[pl.ds(pl.multiple_of(d * HALF + s * BLK + h * PART, PART), PART)]
        n = 8 * h + NX
        over.append(remote(fin.at[h, 1], place, a_ss.at[n], a_rs.at[n], agdev(1, 0)))
        over[-1].start()
        along(h, 0, fin.at[h, 0], place)
        keep.append(pltpu.make_async_copy(fin.at[h, 0], place, l_sem.at[2 + h]))
        keep[-1].start()

    def relay(h):
        over[h].wait_recv()
        place = cg.at[pl.ds(pl.multiple_of((1 - d) * HALF + s * BLK + h * PART, PART), PART)]
        along(h, 1, place, place)

    spread(0)
    spread(1)
    relay(0)
    pass_on(0, 0)

    for cp in gzs:
        cp.wait_recv()
    for i in range(NZ - 1):
        part = part + g_z[i].astype(F32)
    lg_src[...] = part.astype(BF)
    lg[1 + mine] = lg_src[...]
    back = [
        remote(lg_src, lg.at[1 + mine], lg_ss.at[n], lg_rs.at[n], coldev(i))
        for n, i in enumerate((1, 4, 5))
    ]
    edges = []
    for n, (e, to) in enumerate(((1, 0), (NX - 1, BAND + 1))):
        edges.append([
            remote(lg_src, lg.at[to], e_ss.at[n * 4 + i], e_rs.at[n], edgedev(e, i)) for i in range(4)
        ])
    edge_row = (BAND - 1, 0)
    for n in range(2):

        @pl.when(mine == edge_row[n])
        def _():
            for cp in edges[n]:
                cp.start()

    for cp in back:
        cp.start()
    pass_on(1, 0)
    relay(1)
    pass_on(0, 1)
    for cp in back + [edges[0][0], edges[1][0]]:
        cp.wait_recv()

    @pl.when(s == 0)
    def _():
        lg[0] = jnp.zeros((OWN, D), BF)

    @pl.when(s == NX - 1)
    def _():
        lg[BAND + 1] = jnp.zeros((OWN, D), BF)

    def back_taps(b):
        acc = None
        for a in range(3):
            la = lg[2 - a:2 - a + BAND].reshape(ROWS, D)
            t = nt(la, cw[a, b])
            acc = t if acc is None else acc + t
        return acc

    grad = back_taps(1) + shifted(back_taps(0), -1) + shifted(back_taps(2), 1)
    for h in range(BAND):
        fg[:, h] = grad[h * OWN:(h + 1) * OWN].astype(BF).reshape(IMG, LW, CIN)
    for n in range(2):

        @pl.when(mine == edge_row[n])
        def _():
            for cp in edges[n]:
                cp.wait_send()

    for cp in halo + give_u + give_t + col + zs + ring + direct + summed + gcol + gzs + back + over + list(sides_out.values()):
        cp.wait_send()
    for cp in keep + out:
        cp.wait()


def finish_kernel(factor, cg, fg, out_cg, out_fg, wide, sem):
    parts = wide.shape[0]
    rows = CODES // parts
    gives = [pltpu.make_async_copy(fg, out_fg, sem.at[parts])]
    gives[0].start()
    for n in range(parts):
        at = pl.ds(n * rows, rows)
        wide[n] = cg[at, :].astype(F32) * factor
        gives.append(pltpu.make_async_copy(wide.at[n], out_cg.at[at], sem.at[n]))
        gives[-1].start()
    for cp in gives:
        cp.wait()


def finish(cg, fg, factor):
    parts = 4
    hbm = pl.BlockSpec(memory_space=pl.ANY)
    return pl.pallas_call(
        functools.partial(finish_kernel, factor),
        out_shape=(
            jax.ShapeDtypeStruct(cg.shape, F32),
            jax.ShapeDtypeStruct(fg.shape, BF),
        ),
        in_specs=[pl.BlockSpec(memory_space=pltpu.VMEM)] * 2,
        out_specs=(hbm, hbm),
        scratch_shapes=[
            pltpu.VMEM((parts, CODES // parts, HD), F32),
            pltpu.SemaphoreType.DMA((parts + 1,)),
        ],
        compiler_params=pltpu.CompilerParams(vmem_limit_bytes=40 << 20),
        name="widen",
    )(cg, fg)


def on_device(features, conv_weight, codebook, recon_grad):
    dma = pltpu.SemaphoreType.DMA
    vm = pltpu.VMEM
    hbm = pl.BlockSpec(memory_space=pl.ANY)
    sems = [12, 2, 2, 2, 2, 8, 8, 7, 7, 7, 7, 4, 4, 4, 4, 4, 4, 24, 24, 7, 7, 7, 7, 3, 3, 8, 2]
    cg, fg = pl.pallas_call(
        kernel,
        out_shape=(
            pltpu.VMEM((CODES, HD), BF),
            pltpu.VMEM((IMG, BAND, LW, CIN), BF),
        ),
        in_specs=[hbm] * 4,
        out_specs=(pl.BlockSpec(memory_space=pltpu.VMEM), pl.BlockSpec(memory_space=pltpu.VMEM)),
        scratch_shapes=[
            vm((BAND + 2, IMG, LW, CIN), BF),
            vm((3, 3, CIN, D), BF),
            vm((HALF, D), F32),
            vm((HALF, D), BF),
            vm((HALF, D), BF),
            vm((4 * ROWS // LW, LW, D), BF),
            vm((2 * ROWS // LW, LW, D), BF),
            vm((HALF, 2 * ROWS), F32),
            vm((HALF, 2 * ROWS), F32),
            vm((NX, 1, 2 * ROWS), F32),
            vm((PART, 4 * ROWS), BF),
            vm((HALF, 2 * ROWS), BF),
            vm((HALF, 2 * ROWS), BF),
            vm((D, 2 * ROWS), F32),
            vm((D, 2 * ROWS), F32),
            vm((8, 128), F32),
            vm((7, 8, 128), F32),
            vm((NZ, 8, 128), F32),
            vm((4, QTR, D), BF),
            vm((4, PART, D), BF),
            vm((4, QTR, D), F32),
            vm((4, QTR, D), BF),
            vm((2, PART, D), BF),
            vm((2, PART, D), BF),
            vm((2, PART, D), F32),
            vm((2, 2, PART, HD), BF),
            vm((D, HALF), BF),
            vm((2 * ROWS, D), BF),
            vm((7, OWN, D), BF),
            vm((OWN, D), BF),
            vm((NZ - 1, OWN, D), BF),
            vm((OWN, D), BF),
            vm((BAND + 2, OWN, D), BF),
        ] + [dma((n,)) for n in sems] + [pltpu.SemaphoreType.REGULAR((2,))],
        compiler_params=pltpu.CompilerParams(
            collective_id=0, has_side_effects=True, vmem_limit_bytes=58 << 20
        ),
        cost_estimate=pl.CostEstimate(
            flops=12 * 2**30, bytes_accessed=10 << 20, transcendentals=1 << 21
        ),
        name="soft_quantize",
    )(features, conv_weight, codebook, recon_grad)
    entries_all = codebook.shape[0] * lax.axis_size("code")
    rows_all = ROWS * lax.axis_size("dp") * lax.axis_size("spatial")
    return finish(cg, fg, entries_all / rows_all)


def solution(mesh):
    placed = (P("dp", "spatial", None, None), P(), P("code", None), P("dp", "spatial", None, None))
    return jax.shard_map(
        on_device,
        mesh=mesh,
        in_specs=placed,
        out_specs=(P("code", "dp"), P("dp", "spatial", None, None)),
        check_vma=False,
    )
```
